256 devices in a mesh: lat: 16 (over x, y), lon: 16 (over z, core).
Axes of the slice: x: 4, y: 4, z: 8, core: 2. Of those that a mesh axis runs over, the one named last changes fastest.
Arguments:
- fields: float32 [4, 8, 1024, 2048], P(None, None, 'lat', 'lon'), may hold values from -6 to 6
- hyper_coef: float32 [4, 8], replicated, may hold values from 0.004 to 0.03
- vert_coef: float32 [4, 7], replicated, may hold values from 0.2 to 5
- dep_owner: int32 [16, 16, 8, 1], P('lat', 'lon'), may hold values from 0 to 15, as said below
- dep_row: int32 [16, 16, 8, 1], P('lat', 'lon'), may hold values from 0 to 2
- dep_col: int32 [16, 16, 8, 1], P('lat', 'lon'), may hold values from 0 to 3
- shifts: int32 [16, 16, 8, 2], P('lat', 'lon'), may hold values from 1 to 29
- fracs: int32 [16, 16, 8, 2], P('lat', 'lon'), may hold values from 0 to 15
Outputs:
- advected: float32 [4, 8, 1024, 2048], P(None, None, 'lat', 'lon')
The draws below stay inside these ranges and needn't reach their ends.
Inputs may be any that keep to these rules, and one draw needn't show every extreme that they name: `dep_owner`: among the 8 arrival tiles of one device, no value is named more than 2 times, and every device names some value exactly 2 times. In the first and last latitude band the values may be any longitude index; in every other band they lie within 2 of the device's own longitude index, counted around the circle.
All inputs are finite; a program needn't handle non-finite values.
Results may differ from the reference program's by a relative error of at most 0.00007.
Values sent between devices are 32-bit elements; how exact they have to be, the bound alone decides.
No kernel may reach another device: no remote copies, remote signals or barrier semaphores. Data moves between devices by JAX's collectives and lax.ppermute only.
A program may use at most 128 MiB of HBM per device.

```python
import math
import jax
import jax.numpy as jnp
from jax import lax

FIELDS = 4
LEV = 8
TILE = 32
TILE_ROWS = 2
TILE_COLS = 4
CAP = 2
FRACS = 16
LAT_TILES = 32
NLAT = 1024
NLON = 2048
N_LAT = 16
N_LON = 16


def owner_list(dev_key, band, lon_index):
    tile_count = TILE_ROWS * TILE_COLS
    slot_count = N_LON * CAP
    first_key, second_key, third_key = jax.random.split(dev_key, 3)
    order = jax.random.permutation(first_key, slot_count).astype(jnp.int32)
    group = jnp.arange(slot_count, dtype=jnp.int32) // CAP
    polar = (band == 0) | (band == N_LAT - 1)
    reach = jnp.where(polar, N_LON, 5).astype(jnp.int32)
    forced = jax.random.randint(second_key, (), 0, reach, dtype=jnp.int32)
    barred = jnp.logical_and(jnp.logical_not(polar), group >= 5).astype(jnp.int32)
    favoured = (group == forced).astype(jnp.int32)
    score = order + slot_count * barred - slot_count * favoured
    chosen = jnp.argsort(score, stable=True)[:tile_count].astype(jnp.int32)
    chosen_group = chosen // CAP
    owners = jnp.where(polar, chosen_group, (lon_index + chosen_group - 2) % N_LON).astype(jnp.int32)
    shuffle = jax.random.permutation(third_key, tile_count)
    return owners[shuffle]


def draw_dep_owner(key, part):
    key = jax.random.fold_in(key, 11)
    dev_keys = jax.random.split(key, N_LAT * N_LON)
    bands = jnp.repeat(jnp.arange(N_LAT, dtype=jnp.int32), N_LON)
    lon_ids = jnp.tile(jnp.arange(N_LON, dtype=jnp.int32), N_LAT)
    owners = jax.vmap(owner_list)(dev_keys, bands, lon_ids)
    return owners.reshape(N_LAT, N_LON, TILE_ROWS * TILE_COLS, 1).astype(jnp.int32)


def set_ends(entries, own_key, low, largest):
    shape = entries.shape
    index_at = [jax.random.randint(jax.random.fold_in(own_key, axis), (), 0, shape[axis]) for axis in range(len(shape))]
    entries = entries.at[tuple(index_at)].set(low)
    longest = shape.index(max(shape))
    index_at[longest] = (index_at[longest] + 1) % shape[longest]
    return entries.at[tuple(index_at)].set(largest)


def shard_levels(own_key, dims, cuts, smallest, top_value):
    level = 1.0
    for position, blocks in cuts:
        heights = jax.random.uniform(jax.random.fold_in(jax.random.fold_in(own_key, 6), position), (blocks,), jnp.float32, smallest / len(cuts), top_value / len(cuts))
        level = level * jnp.repeat(jnp.exp(heights), dims[position] // blocks).reshape((-1,) + (1,) * (len(dims) - 1 - position))
    return level


def noise(stream_key, extent, spread, most, cuts=(), held_as=jnp.bfloat16):
    drawn = spread * jax.random.normal(stream_key, extent, jnp.float32)
    if cuts:
        drawn = drawn * shard_levels(stream_key, extent, cuts, -0.22, 0.18)
    return jnp.clip(drawn, -most, most).astype(held_as)


def setup_inputs(seed: int = 0) -> dict:
    seeds = jax.random.split(jax.random.key(seed), 9)
    return {
        "fields": noise(seeds[0], (FIELDS, LEV, NLAT, NLON), 1.0, 6.0, ((2, 16), (3, 16)), jnp.float32),
        "hyper_coef": jnp.clip(jnp.exp(jax.random.uniform(seeds[1], (FIELDS, LEV), jnp.float32, math.log(0.004), math.log(0.03))), 0.004, 0.03),
        "vert_coef": jnp.clip(jnp.exp(jax.random.uniform(seeds[2], (FIELDS, LEV - 1), jnp.float32, math.log(0.2), math.log(5.0))), 0.2, 5.0),
        "dep_owner": draw_dep_owner(jax.random.fold_in(seeds[8], 71), 0),
        "dep_row": set_ends(jax.random.randint(seeds[4], (N_LAT, N_LON, TILE_ROWS * TILE_COLS, 1), 0, TILE_ROWS + 1), jax.random.fold_in(seeds[4], 1), 0, TILE_ROWS).astype(jnp.int32),
        "dep_col": set_ends(jax.random.randint(seeds[5], (N_LAT, N_LON, TILE_ROWS * TILE_COLS, 1), 0, TILE_COLS), jax.random.fold_in(seeds[5], 1), 0, TILE_COLS - 1).astype(jnp.int32),
        "shifts": set_ends(jax.random.randint(seeds[6], (N_LAT, N_LON, TILE_ROWS * TILE_COLS, 2), 1, TILE - 2), jax.random.fold_in(seeds[6], 1), 1, (TILE - 2) - 1).astype(jnp.int32),
        "fracs": set_ends(jax.random.randint(seeds[7], (N_LAT, N_LON, TILE_ROWS * TILE_COLS, 2), 0, FRACS), jax.random.fold_in(seeds[7], 1), 0, FRACS - 1).astype(jnp.int32),
    }


HIGHEST_PRECISION = lax.Precision.HIGHEST


def cubic_weights(fraction_index):
    fraction = fraction_index.astype(jnp.float32) / FRACS
    return jnp.stack([
        -fraction * (fraction - 1.0) * (fraction - 2.0) / 6.0,
        (fraction + 1.0) * (fraction - 1.0) * (fraction - 2.0) / 2.0,
        -(fraction + 1.0) * fraction * (fraction - 2.0) / 2.0,
        (fraction + 1.0) * fraction * (fraction - 1.0) / 6.0], axis=-1)


def stencil_matrix(weights):
    row_ids = jnp.arange(TILE, dtype=jnp.int32)[:, None]
    col_ids = jnp.arange(TILE + 3, dtype=jnp.int32)[None, :]
    offset = col_ids - row_ids
    matrix = jnp.zeros(weights.shape[:-1] + (TILE, TILE + 3), jnp.float32)
    for step_index in range(4):
        matrix = matrix + weights[..., step_index, None, None] * (offset == step_index).astype(jnp.float32)
    return matrix


def laplacian(field_values):
    lat_padded = jnp.pad(field_values, ((0, 0), (0, 0), (1, 1), (0, 0)))
    beside = lat_padded[:, :, 2:, :] + lat_padded[:, :, :-2, :] + jnp.roll(field_values, 1, axis=3) + jnp.roll(field_values, -1, axis=3)
    return beside - 4.0 * field_values


def vertical_solve(psi_field, vert_coef):
    fcount = psi_field.shape[0]
    levels = psi_field.shape[1]
    zero_column = jnp.zeros((fcount, 1), jnp.float32)
    lower_coef = jnp.concatenate([zero_column, vert_coef], axis=1)
    upper_coef = jnp.concatenate([vert_coef, zero_column], axis=1)
    diagonal = 1.0 + lower_coef + upper_coef
    sweep_upper = []
    sweep_rhs = []
    for level_index in range(levels):
        lower_now = lower_coef[:, level_index][:, None, None]
        if level_index == 0:
            denominator = diagonal[:, 0][:, None, None]
            rhs_now = psi_field[:, 0]
        else:
            denominator = diagonal[:, level_index][:, None, None] + lower_now * sweep_upper[-1]
            rhs_now = psi_field[:, level_index] + lower_now * sweep_rhs[-1]
        sweep_upper.append(-upper_coef[:, level_index][:, None, None] / denominator)
        sweep_rhs.append(rhs_now / denominator)
    solution = [sweep_rhs[-1]]
    for level_index in range(levels - 2, -1, -1):
        solution.insert(0, sweep_rhs[level_index] - sweep_upper[level_index] * solution[0])
    return jnp.stack(solution, axis=1)


def interpolate_one(window, frac_row, frac_col):
    weight_rows = stencil_matrix(cubic_weights(frac_row))
    weight_cols = stencil_matrix(cubic_weights(frac_col))
    column_pass = jnp.einsum('flab,jb->flaj', window, weight_cols, precision=HIGHEST_PRECISION)
    return jnp.einsum('ia,flaj->flij', weight_rows, column_pass, precision=HIGHEST_PRECISION)


def reference(fields, hyper_coef, vert_coef, dep_owner, dep_row, dep_col, shifts, fracs):
    window_size = TILE + 3
    wrapped = jnp.concatenate([fields, fields[:, :, :, :TILE]], axis=3)
    band_index = jnp.broadcast_to(jnp.arange(N_LAT, dtype=jnp.int32)[:, None, None], dep_row.shape[:3]).reshape(-1)
    owners = dep_owner.reshape(-1)
    dep_tile = jnp.clip(band_index * TILE_ROWS - 1 + dep_row.reshape(-1), 0, LAT_TILES - 2)
    row_start = (TILE * dep_tile + shifts[..., 0].reshape(-1) - 1).astype(jnp.int32)
    col_start = (TILE * (owners * TILE_COLS + dep_col.reshape(-1)) + shifts[..., 1].reshape(-1) - 1).astype(jnp.int32)
    frac_rows = fracs[..., 0].reshape(-1)
    frac_cols = fracs[..., 1].reshape(-1)
    zero_index = jnp.zeros((), jnp.int32)

    def one_tile(packed):
        start_row, start_col, frac_row, frac_col = packed
        window = lax.dynamic_slice(wrapped, (zero_index, zero_index, start_row, start_col), (FIELDS, LEV, window_size, window_size))
        return interpolate_one(window, frac_row, frac_col)

    tile_values = lax.map(one_tile, (row_start, col_start, frac_rows, frac_cols))
    tile_values = tile_values.reshape(N_LAT, N_LON, TILE_ROWS, TILE_COLS, FIELDS, LEV, TILE, TILE)
    phi_field = tile_values.transpose(4, 5, 0, 2, 6, 1, 3, 7).reshape(FIELDS, LEV, NLAT, NLON)
    psi_field = phi_field - hyper_coef[:, :, None, None] * laplacian(laplacian(phi_field))
    return vertical_solve(psi_field, vert_coef)
```

```python
import functools

import jax
import jax.numpy as jnp
from jax import lax
from jax.experimental import pallas as pl
from jax.experimental.pallas import tpu as pltpu
from jax.sharding import Mesh, PartitionSpec as P

TILE = 32
FRACS = 16
LANES = 128
INFO_ROWS = 8
PAIR = 2


def cubic_weights(fraction_index):
    fraction = fraction_index.astype(jnp.float32) / FRACS
    return (
        -fraction * (fraction - 1.0) * (fraction - 2.0) / 6.0,
        (fraction + 1.0) * (fraction - 1.0) * (fraction - 2.0) / 2.0,
        -(fraction + 1.0) * fraction * (fraction - 2.0) / 2.0,
        (fraction + 1.0) * fraction * (fraction - 1.0) / 6.0,
    )


def pack_kernel(tile_cols, row_limits, fields_ref, place_ref, owner_ref, row_ref, col_ref, shifts_ref, fracs_ref, out_ref):
    cells = fields_ref.shape[1]
    out_ref[:, :cells, :] = fields_ref[...]
    first_row = place_ref[0]
    group_row = place_ref[1]
    shape = (INFO_ROWS, LANES)
    lane = lax.broadcasted_iota(jnp.int32, shape, 1)
    tile = lax.broadcasted_iota(jnp.int32, shape, 0)

    def wide(value):
        return jnp.broadcast_to(value, shape)

    dep_tile = jnp.clip(first_row + wide(row_ref[...]), row_limits[0], row_limits[1])
    row_start = TILE * (dep_tile - group_row) + wide(shifts_ref[:, 0:1]) - 1
    dep_col = wide(col_ref[...])
    last = (dep_col == tile_cols - 1).astype(jnp.int32)
    chunk = wide(owner_ref[...]) + last * row_limits[2]
    lane_start = TILE * (dep_col - last) + wide(shifts_ref[:, 1:2]) - 1
    turn = LANES + TILE * lax.rem(tile, tile_cols) - lane_start
    info = jnp.where(lane == 0, row_start, jnp.where(lane == 1, chunk, turn)).astype(jnp.float32)
    for which in range(2):
        weights = cubic_weights(wide(fracs_ref[:, which : which + 1]))
        for tap in range(4):
            info = jnp.where(lane == 3 + 4 * which + tap, weights[tap], info)
    for block in range(out_ref.shape[0]):
        out_ref[block, cells:, :] = info


def interpolate_kernel(info_ref, blocks_ref, north_ref, south_ref, phi_ref, top_ref, bottom_ref, ext_ref, sem):
    chunks, halo = north_ref.shape[0], north_ref.shape[1]
    cells = phi_ref.shape[1] // PAIR
    tile_rows = cells // TILE
    tile_cols = LANES // TILE
    copies = [
        pltpu.make_async_copy(north_ref, ext_ref.at[0:chunks, 0:halo, :], sem.at[0]),
        pltpu.make_async_copy(south_ref, ext_ref.at[0:chunks, halo + PAIR * cells : 2 * halo + PAIR * cells, :], sem.at[1]),
    ]
    for band in range(PAIR):
        copies.append(
            pltpu.make_async_copy(
                blocks_ref.at[band * chunks : (band + 1) * chunks, 0:cells, :],
                ext_ref.at[0:chunks, halo + band * cells : halo + (band + 1) * cells, :],
                sem.at[2 + band],
            )
        )
    for copy in copies:
        copy.start()
    for copy in copies:
        copy.wait()
    rows = ext_ref.shape[1]
    lane_rows = lax.broadcasted_iota(jnp.int32, (rows, LANES), 1)

    def shifted(chunk, carry):
        after = lax.rem(chunk + 1, chunks)
        mixed = jnp.where(lane_rows < TILE, ext_ref[after], ext_ref[chunk])
        ext_ref[chunks + chunk] = pltpu.roll(mixed, LANES - TILE, 1)
        return carry

    lax.fori_loop(0, chunks, shifted, 0)
    lane = lax.broadcasted_iota(jnp.int32, (TILE, LANES), 1)
    group = lane // TILE

    def one_device(device, carry):
        band = device // chunks
        chunk_out = lax.rem(device, chunks)
        for tile_row in range(tile_rows):
            taps = [None] * 4
            col_weights = [None] * 4
            for tile_col in range(tile_cols):
                tile = tile_row * tile_cols + tile_col
                base = tile * 16
                start = info_ref[device, base].astype(jnp.int32)
                source = info_ref[device, base + 1].astype(jnp.int32)
                turn = info_ref[device, base + 2].astype(jnp.int32)
                total = None
                for tap in range(4):
                    part = info_ref[device, base + 3 + tap] * ext_ref[source, pl.ds(start + tap, TILE), :]
                    total = part if total is None else total + part
                for tap in range(4):
                    turned = pltpu.roll(total, lax.bitwise_and(turn - tap, LANES - 1), 1)
                    weight = jnp.full((1, LANES), info_ref[device, base + 7 + tap], jnp.float32)
                    if tile_col == 0:
                        taps[tap] = turned
                        col_weights[tap] = weight
                    else:
                        here = group == tile_col
                        taps[tap] = jnp.where(here, turned, taps[tap])
                        col_weights[tap] = jnp.where(here[0:1], weight, col_weights[tap])
            value = col_weights[0] * taps[0]
            for tap in range(1, 4):
                value = value + col_weights[tap] * taps[tap]
            phi_ref[chunk_out, pl.ds(band * cells + tile_row * TILE, TILE), :] = value
        return carry

    lax.fori_loop(0, PAIR * chunks, one_device, 0)
    for chunk in range(chunks):
        top_ref[2 * chunk : 2 * chunk + 2, :] = phi_ref[chunk, 0:2, :]
        bottom_ref[2 * chunk : 2 * chunk + 2, :] = phi_ref[chunk, PAIR * cells - 2 : PAIR * cells, :]


PAD = 16


def diffuse_kernel(scalars_ref, phi_ref, north_ref, south_ref, psi_ref, ext_ref, lap_ref):
    chunks, rows = phi_ref.shape[0], phi_ref.shape[1]
    cells = rows // PAIR
    coef, has_north, has_south = scalars_ref[0], scalars_ref[1], scalars_ref[2]

    for chunk in range(chunks):
        ext_ref[chunk, 0:PAD, :] = jnp.zeros((PAD, LANES), jnp.float32)
        ext_ref[chunk, PAD + rows :, :] = jnp.zeros((PAD, LANES), jnp.float32)
        ext_ref[chunk, PAD : PAD + rows, :] = phi_ref[chunk]
        ext_ref[chunk, PAD - 2 : PAD, :] = north_ref[2 * chunk : 2 * chunk + 2, :]
        ext_ref[chunk, PAD + rows : PAD + rows + 2, :] = south_ref[2 * chunk : 2 * chunk + 2, :]

    def laplacian(ref, chunk, first, count):
        lane = lax.broadcasted_iota(jnp.int32, (count, LANES), 1)
        west = lax.rem(chunk + chunks - 1, chunks)
        east = lax.rem(chunk + 1, chunks)
        here = ref[chunk, first : first + count, :]
        from_west = pltpu.roll(jnp.where(lane == LANES - 1, ref[west, first : first + count, :], here), 1, 1)
        from_east = pltpu.roll(jnp.where(lane == 0, ref[east, first : first + count, :], here), LANES - 1, 1)
        beside = ref[chunk, first + 1 : first + 1 + count, :] + ref[chunk, first - 1 : first - 1 + count, :] + from_west + from_east
        return beside - 4.0 * here

    def first_pass(chunk, carry):
        lap_ref[chunk, PAD - 8 : PAD, :] = laplacian(ext_ref, chunk, PAD - 8, 8) * has_north
        lap_ref[chunk, PAD : PAD + rows, :] = laplacian(ext_ref, chunk, PAD, rows)
        lap_ref[chunk, PAD + rows : PAD + rows + 8, :] = laplacian(ext_ref, chunk, PAD + rows, 8) * has_south
        return carry

    def second_pass(chunk, carry):
        psi = phi_ref[chunk] - coef * laplacian(lap_ref, chunk, PAD, rows)
        for band in range(PAIR):
            psi_ref[band * chunks + chunk] = psi[band * cells : (band + 1) * cells]
        return carry

    lax.fori_loop(0, chunks, first_pass, 0)
    lax.fori_loop(0, chunks, second_pass, 0)


def vertical_kernel(levels, lower_ref, upper_ref, inverse_ref, psi_ref, out_ref):
    field = pl.program_id(0)
    sweep = []
    for level in range(levels):
        rhs = psi_ref[level]
        if level:
            rhs = rhs + lower_ref[field, level] * sweep[-1]
        sweep.append(rhs * inverse_ref[field, level])
    value = sweep[-1]
    out_ref[0, levels - 1] = value
    for level in range(levels - 2, -1, -1):
        value = sweep[level] - upper_ref[field, level] * value
        out_ref[0, level] = value


def vertical_tables(vert_coef):
    fcount = vert_coef.shape[0]
    levels = vert_coef.shape[1] + 1
    zero_column = jnp.zeros((fcount, 1), jnp.float32)
    lower_coef = jnp.concatenate([zero_column, vert_coef], axis=1)
    upper_coef = jnp.concatenate([vert_coef, zero_column], axis=1)
    diagonal = 1.0 + lower_coef + upper_coef
    uppers, inverses = [], []
    for level in range(levels):
        denominator = diagonal[:, level]
        if level:
            denominator = denominator + lower_coef[:, level] * uppers[-1]
        inverses.append(1.0 / denominator)
        uppers.append(-upper_coef[:, level] / denominator)
    return lower_coef, jnp.stack(uppers, axis=1), jnp.stack(inverses, axis=1)


SMEM = pltpu.MemorySpace.SMEM
VMEM = pltpu.MemorySpace.VMEM


def smem():
    return pl.BlockSpec(memory_space=SMEM)


def vmem():
    return pl.BlockSpec(memory_space=VMEM)


def anywhere():
    return pl.BlockSpec(memory_space=pl.ANY)


def body(fields, hyper_coef, vert_coef, dep_owner, dep_row, dep_col, shifts, fracs):
    fcount, levels, cells, width = fields.shape
    count = fcount * levels
    chunks = lax.axis_size("lon")
    groups = lax.axis_size("group")
    tile_rows = cells // TILE
    tile_cols = width // TILE
    tiles = tile_rows * tile_cols
    group = lax.axis_index("group")
    band = group * PAIR + lax.axis_index("part")
    rows = PAIR * cells
    f32 = jnp.float32
    limit = pltpu.CompilerParams(vmem_limit_bytes=48 * 1024 * 1024)

    place = jnp.stack([band * tile_rows - 1, group * PAIR * tile_rows - 1]).astype(jnp.int32)
    blocks = pl.pallas_call(
        functools.partial(pack_kernel, tile_cols, (0, groups * PAIR * tile_rows - 2, chunks)),
        out_shape=jax.ShapeDtypeStruct((count, cells + INFO_ROWS, width), f32),
        in_specs=[vmem(), smem(), vmem(), vmem(), vmem(), vmem(), vmem()],
        out_specs=vmem(),
        compiler_params=limit,
    )(
        fields.reshape(count, cells, width),
        place,
        dep_owner.reshape(tiles, 1),
        dep_row.reshape(tiles, 1),
        dep_col.reshape(tiles, 1),
        shifts.reshape(tiles, 2),
        fracs.reshape(tiles, 2),
    )
    blocks = lax.all_to_all(blocks, ("part", "lon"), 0, 0, tiled=True)
    southward = [(i, i + 1) for i in range(groups - 1)]
    northward = [(i + 1, i) for i in range(groups - 1)]
    north = lax.ppermute(blocks[(PAIR - 1) * chunks :, cells - TILE : cells, :], "group", southward)
    south = lax.ppermute(blocks[:chunks, :TILE, :], "group", northward)
    info = blocks[:, cells : cells + tiles, :16].reshape(PAIR * chunks, tiles * 16)
    edge = jax.ShapeDtypeStruct((2 * chunks, width), f32)
    phi, top, bottom = pl.pallas_call(
        interpolate_kernel,
        out_shape=(jax.ShapeDtypeStruct((chunks, rows, width), f32), edge, edge),
        in_specs=[smem(), anywhere(), anywhere(), anywhere()],
        out_specs=(vmem(), vmem(), vmem()),
        scratch_shapes=[
            pltpu.VMEM((2 * chunks, rows + 2 * TILE, width), f32),
            pltpu.SemaphoreType.DMA((2 + PAIR,)),
        ],
        compiler_params=limit,
    )(info, blocks, north, south)
    above = lax.ppermute(bottom, "group", southward)
    below = lax.ppermute(top, "group", northward)
    member = lax.axis_index("part") * chunks + lax.axis_index("lon")
    scalars = jnp.stack(
        [
            lax.dynamic_index_in_dim(hyper_coef.reshape(-1), member, 0, keepdims=False),
            (group > 0).astype(f32),
            (group < groups - 1).astype(f32),
        ]
    )
    psi = pl.pallas_call(
        diffuse_kernel,
        out_shape=jax.ShapeDtypeStruct((count, cells, width), f32),
        in_specs=[smem(), vmem(), vmem(), vmem()],
        out_specs=vmem(),
        scratch_shapes=[
            pltpu.VMEM((chunks, rows + 2 * PAD, width), f32),
            pltpu.VMEM((chunks, rows + 2 * PAD, width), f32),
        ],
        compiler_params=limit,
    )(scalars, phi, above, below)
    psi = lax.all_to_all(psi, ("part", "lon"), 0, 0, tiled=True)
    lower, upper, inverse = vertical_tables(vert_coef)
    return pl.pallas_call(
        functools.partial(vertical_kernel, levels),
        grid=(fcount,),
        out_shape=jax.ShapeDtypeStruct((fcount, levels, cells, width), f32),
        in_specs=[
            smem(),
            smem(),
            smem(),
            pl.BlockSpec((levels, cells, width), lambda field: (field, 0, 0)),
        ],
        out_specs=pl.BlockSpec((1, levels, cells, width), lambda field: (field, 0, 0, 0)),
        compiler_params=limit,
    )(lower, upper, inverse, psi)


def solution(mesh):
    lat, lon = mesh.shape["lat"], mesh.shape["lon"]
    grouped = Mesh(mesh.devices.reshape(lat // PAIR, PAIR, lon), ("group", "part", "lon"))
    bands = ("group", "part")
    cells = P(None, None, bands, "lon")
    tiles = P(bands, "lon", None, None)
    return jax.shard_map(
        body,
        mesh=grouped,
        in_specs=(cells, P(), P(), tiles, tiles, tiles, tiles, tiles),
        out_specs=cells,
        check_vma=False,
    )
```

```python
import functools

import jax
import jax.numpy as jnp
from jax import lax
from jax.experimental import pallas as pl
from jax.experimental.pallas import tpu as pltpu
from jax.sharding import Mesh, PartitionSpec as P

TILE = 32
FRACS = 16
LANES = 128
INFO_ROWS = 8
PAIR = 2
TAPS = 4
SPAN = 40


def cubic_weights(fraction_index):
    fraction = fraction_index.astype(jnp.float32) / FRACS
    return (
        -fraction * (fraction - 1.0) * (fraction - 2.0) / 6.0,
        (fraction + 1.0) * (fraction - 1.0) * (fraction - 2.0) / 2.0,
        -(fraction + 1.0) * fraction * (fraction - 2.0) / 2.0,
        (fraction + 1.0) * fraction * (fraction - 1.0) / 6.0,
    )


def swapped():
    return lax.rem(lax.axis_index("group"), 2)


def pack_kernel(
    tile_rows, tile_cols, last_row, fields_ref, owner_ref, row_ref, col_ref, shifts_ref, fracs_ref, out_ref, table_ref, sem
):
    count, cells = fields_ref.shape[0], fields_ref.shape[1]
    half = count // PAIR
    swap = swapped()
    copies = []
    for part in range(PAIR):
        source = lax.bitwise_xor(part, swap) * half
        copies.append(
            pltpu.make_async_copy(
                fields_ref.at[pl.ds(source, half)], out_ref.at[part * half : (part + 1) * half, 0:cells, :], sem.at[part]
            )
        )
    for copy in copies:
        copy.start()
    tiles = owner_ref.shape[1]
    group = lax.axis_index("group")
    band = group * PAIR + lax.axis_index("part")
    table_ref[...] = jnp.zeros(table_ref.shape, jnp.int32)
    table_ref[0:1, 0:tiles] = owner_ref[...]
    table_ref[1:2, 0:tiles] = row_ref[...]
    table_ref[2:3, 0:tiles] = col_ref[...]
    table_ref[3:5, 0:tiles] = shifts_ref[...]
    table_ref[5:7, 0:tiles] = fracs_ref[...]
    table = table_ref[...]
    owner, dep_row, dep_col = table[0:1], table[1:2], table[2:3]
    shift_row, shift_col, frac_row, frac_col = table[3:4], table[4:5], table[5:6], table[6:7]
    dep_tile = jnp.clip(band * tile_rows - 1 + dep_row, 0, last_row)
    start = TILE * (dep_tile - (group * PAIR * tile_rows - 1)) + shift_row - 1
    column = TILE * dep_col + shift_col - 1
    wrapped = jnp.where(dep_col == tile_cols - 1, TILE, 0)
    position = lax.rem(lax.broadcasted_iota(jnp.int32, (1, LANES), 1), tile_cols)
    turn = lax.bitwise_and(LANES + TILE * position - column, LANES - 1)
    shape = (INFO_ROWS, LANES)
    index = lax.broadcasted_iota(jnp.int32, shape, 0)
    lane = lax.broadcasted_iota(jnp.int32, shape, 1)
    info = jnp.zeros(shape, jnp.float32)
    for place, value in enumerate(cubic_weights(frac_row) + cubic_weights(frac_col)):
        info = jnp.where(index == place, value, info)
    places = jnp.zeros(shape, jnp.int32)
    for place, value in enumerate((start, owner, wrapped, turn)):
        places = jnp.where(index == place, value, places)
    info = jnp.where(lane < tiles, info, pltpu.roll(places.astype(jnp.float32), tiles, 1))
    for block in range(count):
        out_ref[block, cells:, :] = info
    for copy in copies:
        copy.wait()


def interpolate_kernel(
    places_ref, blocks_ref, north_ref, south_ref, phi_ref, top_ref, bottom_ref, ext_ref, pass_ref, sem
):
    chunks, halo = north_ref.shape[0], north_ref.shape[1]
    cells = phi_ref.shape[1] // PAIR
    tile_rows = cells // TILE
    tile_cols = LANES // TILE
    tiles = tile_rows * tile_cols
    copies = [
        pltpu.make_async_copy(north_ref, ext_ref.at[:, 0:halo, :], sem.at[0]),
        pltpu.make_async_copy(south_ref, ext_ref.at[:, halo + PAIR * cells : 2 * halo + PAIR * cells, :], sem.at[1]),
    ]
    for band in range(PAIR):
        copies.append(
            pltpu.make_async_copy(
                blocks_ref.at[band * chunks : (band + 1) * chunks, 0:cells, :],
                ext_ref.at[:, halo + band * cells : halo + (band + 1) * cells, :],
                sem.at[2 + band],
            )
        )
    for copy in copies:
        copy.start()
    for copy in copies:
        copy.wait()
    lane = lax.broadcasted_iota(jnp.int32, (SPAN, LANES), 1)
    lane_info = lax.broadcasted_iota(jnp.int32, (INFO_ROWS, LANES), 1)
    first_even = lane < 48
    first_odd = (lane >= 16) & (lane < 80)
    even_group = [lax.bitwise_and(lane - tap, TILE) == 0 for tap in range(TAPS)]

    def columns(device, tile_row, slot):
        own = lane_info // TILE + tile_row * tile_cols
        weights = jnp.take_along_axis(blocks_ref[device, cells:, :], own, axis=1)

        def window(tile_col):
            tile = tile_row * tile_cols + tile_col
            start, source, wrapped, turn = (places_ref[device, place * tiles + tile] for place in range(4))
            after = lax.rem(source + 1, chunks)
            rows = pl.ds(start, SPAN)
            return pltpu.roll(jnp.where(lane < wrapped, ext_ref[after, rows, :], ext_ref[source, rows, :]), turn, 1)

        evens = jnp.where(first_even, window(0), window(2))
        odds = jnp.where(first_odd, window(1), window(3))
        total = None
        for tap in range(TAPS):
            value = jnp.where(even_group[tap], evens, odds)
            if tap:
                value = pltpu.roll(value, LANES - tap, 1)
            value = weights[TAPS + tap : TAPS + tap + 1] * value
            total = value if total is None else total + value
        pass_ref[slot] = total
        return weights

    def rows_of(device, tile_row, slot, weights):
        band = device // chunks
        total = None
        for tap in range(TAPS):
            value = weights[tap : tap + 1] * pass_ref[slot, tap : tap + TILE, :]
            total = value if total is None else total + value
        first = pl.multiple_of(band * cells + tile_row * TILE, TILE)
        phi_ref[lax.rem(device, chunks), pl.ds(first, TILE), :] = total

    together = pass_ref.shape[0] // tile_rows

    def step(index, carry):
        work = []
        for place in range(together):
            device = index * together + place
            for tile_row in range(tile_rows):
                slot = place * tile_rows + tile_row
                work.append((device, tile_row, slot, columns(device, tile_row, slot)))
        for item in work:
            rows_of(*item)
        return carry

    lax.fori_loop(0, PAIR * chunks // together, step, 0)
    for chunk in range(chunks):
        top_ref[2 * chunk : 2 * chunk + 2, :] = phi_ref[chunk, 0:2, :]
        bottom_ref[2 * chunk : 2 * chunk + 2, :] = phi_ref[chunk, PAIR * cells - 2 : PAIR * cells, :]


PAD = 8


def laplacian(ref, chunks, chunk, first, count):
    lane = lax.broadcasted_iota(jnp.int32, (count, LANES), 1)
    west = lax.rem(chunk + chunks - 1, chunks)
    east = lax.rem(chunk + 1, chunks)
    here = ref[chunk, first : first + count, :]
    from_west = pltpu.roll(jnp.where(lane == LANES - 1, ref[west, first : first + count, :], here), 1, 1)
    from_east = pltpu.roll(jnp.where(lane == 0, ref[east, first : first + count, :], here), LANES - 1, 1)
    beside = ref[chunk, first + 1 : first + 1 + count, :] + ref[chunk, first - 1 : first - 1 + count, :] + from_west + from_east
    return beside - 4.0 * here


def own_coef(coef_ref, half):
    levels = coef_ref.shape[1]
    member = lax.bitwise_xor(lax.axis_index("part"), swapped()) * half + lax.axis_index("lon")
    return coef_ref[member // levels, lax.rem(member, levels)]


def diffuse_kernel(coef_ref, phi_ref, psi_ref, lap_ref):
    chunks, rows = phi_ref.shape[0], phi_ref.shape[1]
    cells = rows // PAIR
    coef = own_coef(coef_ref, chunks)

    def first_pass(chunk, carry):
        lap_ref[chunk, PAD - 1 : rows - PAD + 1, :] = laplacian(phi_ref, chunks, chunk, PAD - 1, rows - 2 * PAD + 2)
        return carry

    def second_pass(chunk, carry):
        psi = phi_ref[chunk, PAD : rows - PAD, :] - coef * laplacian(lap_ref, chunks, chunk, PAD, rows - 2 * PAD)
        psi_ref[chunk, 0:PAD, :] = jnp.zeros((PAD, LANES), jnp.float32)
        psi_ref[chunk, PAD:, :] = psi[0 : cells - PAD]
        psi_ref[chunks + chunk, 0 : cells - PAD, :] = psi[cells - PAD :]
        psi_ref[chunks + chunk, cells - PAD :, :] = jnp.zeros((PAD, LANES), jnp.float32)
        return carry

    lax.fori_loop(0, chunks, first_pass, 0)
    lax.fori_loop(0, chunks, second_pass, 0)


def mend_kernel(groups, coef_ref, phi_ref, north_ref, south_ref, inner_ref, psi_ref, ext_ref, lap_ref, edge_ref, sem):
    chunks, rows = phi_ref.shape[0], phi_ref.shape[1]
    cells = rows // PAIR
    coef = own_coef(coef_ref, chunks)
    group = lax.axis_index("group")
    has_north = jnp.where(group > 0, 1.0, 0.0)
    has_south = jnp.where(group < groups - 1, 1.0, 0.0)
    zeros = jnp.zeros((PAD, LANES), jnp.float32)

    for side in range(2):
        for chunk in range(chunks):
            place = side * chunks + chunk
            ext_ref[place, 0:PAD, :] = zeros
            ext_ref[place, 4 * PAD :, :] = zeros
            if side == 0:
                ext_ref[place, PAD : 2 * PAD, :] = zeros
                ext_ref[place, 2 * PAD - 2 : 2 * PAD, :] = north_ref[2 * chunk : 2 * chunk + 2, :]
                ext_ref[place, 2 * PAD : 4 * PAD, :] = phi_ref[chunk, 0 : 2 * PAD, :]
            else:
                ext_ref[place, PAD : 3 * PAD, :] = phi_ref[chunk, rows - 2 * PAD :, :]
                ext_ref[place, 3 * PAD : 4 * PAD, :] = zeros
                ext_ref[place, 3 * PAD : 3 * PAD + 2, :] = south_ref[2 * chunk : 2 * chunk + 2, :]
    for side in range(2):
        own = pl.ds(side * chunks, chunks)
        for chunk in range(chunks):
            lap_ref[side * chunks + chunk, PAD : 4 * PAD, :] = laplacian(ext_ref.at[own], chunks, chunk, PAD, 3 * PAD)
        for chunk in range(chunks):
            place = side * chunks + chunk
            if side == 0:
                lap_ref[place, PAD : 2 * PAD, :] = lap_ref[place, PAD : 2 * PAD, :] * has_north
            else:
                lap_ref[place, 3 * PAD : 4 * PAD, :] = lap_ref[place, 3 * PAD : 4 * PAD, :] * has_south
        for chunk in range(chunks):
            twice = laplacian(lap_ref.at[own], chunks, chunk, 2 * PAD, PAD)
            here = phi_ref[chunk, 0:PAD, :] if side == 0 else phi_ref[chunk, rows - PAD :, :]
            edge_ref[side * chunks + chunk] = here - coef * twice
    copies = [
        pltpu.make_async_copy(edge_ref.at[0:chunks], psi_ref.at[0:chunks, 0:PAD, :], sem.at[0]),
        pltpu.make_async_copy(
            edge_ref.at[chunks : 2 * chunks], psi_ref.at[(PAIR - 1) * chunks :, cells - PAD : cells, :], sem.at[1]
        ),
    ]
    for copy in copies:
        copy.start()
    for copy in copies:
        copy.wait()


def vertical_kernel(levels, lower_ref, upper_ref, inverse_ref, psi_ref, out_ref):
    field = pl.program_id(0)
    source = lax.bitwise_xor(field, swapped() * (pl.num_programs(0) // PAIR)) * levels
    sweep = []
    for level in range(levels):
        rhs = psi_ref[source + level]
        if level:
            rhs = rhs + lower_ref[field, level] * sweep[-1]
        sweep.append(rhs * inverse_ref[field, level])
    value = sweep[-1]
    out_ref[0, levels - 1] = value
    for level in range(levels - 2, -1, -1):
        value = sweep[level] - upper_ref[field, level] * value
        out_ref[0, level] = value


def vertical_tables(vert_coef):
    fcount = vert_coef.shape[0]
    levels = vert_coef.shape[1] + 1
    zero_column = jnp.zeros((fcount, 1), jnp.float32)
    lower_coef = jnp.concatenate([zero_column, vert_coef], axis=1)
    upper_coef = jnp.concatenate([vert_coef, zero_column], axis=1)
    diagonal = 1.0 + lower_coef + upper_coef
    uppers, inverses = [], []
    for level in range(levels):
        denominator = diagonal[:, level]
        if level:
            denominator = denominator + lower_coef[:, level] * uppers[-1]
        inverses.append(1.0 / denominator)
        uppers.append(-upper_coef[:, level] / denominator)
    return lower_coef, jnp.stack(uppers, axis=1), jnp.stack(inverses, axis=1)


SMEM = pltpu.MemorySpace.SMEM
VMEM = pltpu.MemorySpace.VMEM


def smem():
    return pl.BlockSpec(memory_space=SMEM)


def vmem():
    return pl.BlockSpec(memory_space=VMEM)


def anywhere():
    return pl.BlockSpec(memory_space=pl.ANY)


def body(fields, hyper_coef, vert_coef, dep_owner, dep_row, dep_col, shifts, fracs):
    fcount, levels, cells, width = fields.shape
    count = fcount * levels
    chunks = lax.axis_size("lon")
    groups = lax.axis_size("group")
    tile_rows = cells // TILE
    tile_cols = width // TILE
    tiles = tile_rows * tile_cols
    rows = PAIR * cells
    f32 = jnp.float32
    limit = pltpu.CompilerParams(vmem_limit_bytes=48 * 1024 * 1024)

    blocks = pl.pallas_call(
        functools.partial(pack_kernel, tile_rows, tile_cols, groups * PAIR * tile_rows - 2),
        out_shape=jax.ShapeDtypeStruct((count, cells + INFO_ROWS, width), f32),
        in_specs=[anywhere(), vmem(), vmem(), vmem(), vmem(), vmem()],
        out_specs=vmem(),
        scratch_shapes=[pltpu.VMEM((8, LANES), jnp.int32), pltpu.SemaphoreType.DMA((PAIR,))],
        compiler_params=limit,
    )(
        fields.reshape(count, cells, width),
        dep_owner.reshape(1, tiles),
        dep_row.reshape(1, tiles),
        dep_col.reshape(1, tiles),
        shifts.reshape(tiles, 2).T,
        fracs.reshape(tiles, 2).T,
    )
    blocks = lax.all_to_all(blocks, ("part", "lon"), 0, 0, tiled=True)
    southward = [
        (group * PAIR + part, (group + 1) * PAIR + PAIR - 1 - part) for group in range(groups - 1) for part in range(PAIR)
    ]
    northward = [(target, source) for source, target in southward]
    bands = ("group", "part")
    north = lax.ppermute(blocks[(PAIR - 1) * chunks :, cells - TILE : cells, :], bands, southward)
    south = lax.ppermute(blocks[:chunks, :TILE, :], bands, northward)
    places = blocks[:, cells : cells + 4, tiles : 2 * tiles].astype(jnp.int32).reshape(PAIR * chunks, 4 * tiles)
    edge = jax.ShapeDtypeStruct((2 * chunks, width), f32)
    phi, top, bottom = pl.pallas_call(
        interpolate_kernel,
        out_shape=(jax.ShapeDtypeStruct((chunks, rows, width), f32), edge, edge),
        in_specs=[smem(), vmem(), vmem(), vmem()],
        out_specs=(vmem(), vmem(), vmem()),
        scratch_shapes=[
            pltpu.VMEM((chunks, rows + 2 * TILE + 8, width), f32),
            pltpu.VMEM((2 * tile_rows, SPAN, width), f32),
            pltpu.SemaphoreType.DMA((2 + PAIR,)),
        ],
        compiler_params=limit,
    )(places, blocks, north, south)
    above = lax.ppermute(bottom, bands, southward)
    below = lax.ppermute(top, bands, northward)
    psi_shape = jax.ShapeDtypeStruct((count, cells, width), f32)
    psi = pl.pallas_call(
        diffuse_kernel,
        out_shape=psi_shape,
        in_specs=[smem(), vmem()],
        out_specs=vmem(),
        scratch_shapes=[pltpu.VMEM((chunks, rows, width), f32)],
        compiler_params=limit,
    )(hyper_coef, phi)
    psi = pl.pallas_call(
        functools.partial(mend_kernel, groups),
        out_shape=psi_shape,
        in_specs=[smem(), vmem(), vmem(), vmem(), anywhere()],
        out_specs=anywhere(),
        input_output_aliases={4: 0},
        scratch_shapes=[
            pltpu.VMEM((2 * chunks, 5 * PAD, width), f32),
            pltpu.VMEM((2 * chunks, 5 * PAD, width), f32),
            pltpu.VMEM((2 * chunks, PAD, width), f32),
            pltpu.SemaphoreType.DMA((2,)),
        ],
        compiler_params=limit,
    )(hyper_coef, phi, above, below, psi)
    psi = lax.all_to_all(psi, ("part", "lon"), 0, 0, tiled=True)
    lower, upper, inverse = vertical_tables(vert_coef)
    return pl.pallas_call(
        functools.partial(vertical_kernel, levels),
        grid=(fcount,),
        out_shape=jax.ShapeDtypeStruct((fcount, levels, cells, width), f32),
        in_specs=[smem(), smem(), smem(), vmem()],
        out_specs=pl.BlockSpec((1, levels, cells, width), lambda field: (field, 0, 0, 0)),
        compiler_params=limit,
    )(lower, upper, inverse, psi)


def solution(mesh):
    lat, lon = mesh.shape["lat"], mesh.shape["lon"]
    grouped = Mesh(mesh.devices.reshape(lat // PAIR, PAIR, lon), ("group", "part", "lon"))
    bands = ("group", "part")
    cells = P(None, None, bands, "lon")
    tiles = P(bands, "lon", None, None)
    return jax.shard_map(
        body,
        mesh=grouped,
        in_specs=(cells, P(), P(), tiles, tiles, tiles, tiles, tiles),
        out_specs=cells,
        check_vma=False,
    )
```

```python
import functools

import jax
import jax.numpy as jnp
from jax import lax
from jax.experimental import pallas as pl
from jax.experimental.pallas import tpu as pltpu
from jax.sharding import PartitionSpec as P

TILE = 32
FRACS = 16
LANES = 128
INFO_ROWS = 8
HALVES = 2
TAPS = 4
SPAN = 40


def cubic_weights(fraction_index):
    fraction = fraction_index.astype(jnp.float32) / FRACS
    return (
        -fraction * (fraction - 1.0) * (fraction - 2.0) / 6.0,
        (fraction + 1.0) * (fraction - 1.0) * (fraction - 2.0) / 2.0,
        -(fraction + 1.0) * fraction * (fraction - 2.0) / 2.0,
        (fraction + 1.0) * fraction * (fraction - 1.0) / 6.0,
    )


def pack_kernel(tile_rows, tile_cols, last_row, fields_ref, table_ref, out_ref, wide_ref, sem):
    count, cells = out_ref.shape[0], fields_ref.shape[1]
    copy = pltpu.make_async_copy(fields_ref.at[0:count], out_ref.at[:, 0:cells, :], sem.at[0])
    copy.start()
    entries, tiles = table_ref.shape
    band = lax.axis_index("lat")
    wide_ref[...] = jnp.zeros(wide_ref.shape, jnp.int32)
    wide_ref[0:entries, 0:tiles] = table_ref[...]
    table = wide_ref[...]
    owner, dep_row, dep_col = table[0:1], table[1:2], table[2:3]
    shift_row, shift_col, frac_row, frac_col = table[3:4], table[4:5], table[5:6], table[6:7]
    dep_tile = jnp.clip(band * tile_rows - 1 + dep_row, 0, last_row)
    start = TILE * (dep_tile - (band * tile_rows - 1)) + shift_row - 1
    column = TILE * dep_col + shift_col - 1
    wrapped = jnp.where(dep_col == tile_cols - 1, TILE, 0)
    position = lax.rem(lax.broadcasted_iota(jnp.int32, (1, LANES), 1), tile_cols)
    turn = lax.bitwise_and(LANES + TILE * position - column, LANES - 1)
    shape = (INFO_ROWS, LANES)
    index = lax.broadcasted_iota(jnp.int32, shape, 0)
    lane = lax.broadcasted_iota(jnp.int32, shape, 1)
    info = jnp.zeros(shape, jnp.float32)
    for place, value in enumerate(cubic_weights(frac_row) + cubic_weights(frac_col)):
        info = jnp.where(index == place, value, info)
    places = jnp.zeros(shape, jnp.int32)
    for place, value in enumerate((start, owner, wrapped, turn)):
        places = jnp.where(index == place, value, places)
    info = jnp.where(lane < tiles, info, pltpu.roll(places.astype(jnp.float32), tiles, 1))
    for block in range(count):
        out_ref[block, cells:, :] = info
    copy.wait()


def interpolate_kernel(
    places_ref, info_ref, blocks_ref, north_ref, south_ref, phi_ref, top_ref, bottom_ref, ext_ref, pass_ref, sem
):
    chunks, halo = north_ref.shape[0], north_ref.shape[1]
    cells = phi_ref.shape[1]
    tile_rows = cells // TILE
    tile_cols = LANES // TILE
    tiles = tile_rows * tile_cols
    copies = [
        pltpu.make_async_copy(north_ref, ext_ref.at[:, 0:halo, :], sem.at[0]),
        pltpu.make_async_copy(blocks_ref.at[:, 0:cells, :], ext_ref.at[:, halo : halo + cells, :], sem.at[1]),
        pltpu.make_async_copy(south_ref, ext_ref.at[:, halo + cells : 2 * halo + cells, :], sem.at[2]),
    ]
    for copy in copies:
        copy.start()
    for copy in copies:
        copy.wait()
    lane = lax.broadcasted_iota(jnp.int32, (SPAN, LANES), 1)
    lane_info = lax.broadcasted_iota(jnp.int32, (INFO_ROWS, LANES), 1)
    first_even = lane < 48
    first_odd = (lane >= 16) & (lane < 80)
    even_group = [lax.bitwise_and(lane - tap, TILE) == 0 for tap in range(TAPS)]

    def columns(device, tile_row, slot):
        own = lane_info // TILE + tile_row * tile_cols
        weights = jnp.take_along_axis(info_ref[device, cells:, :], own, axis=1)

        def window(tile_col):
            tile = tile_row * tile_cols + tile_col
            start, source, wrapped, turn = (places_ref[device, place * tiles + tile] for place in range(4))
            after = lax.rem(source + 1, chunks)
            rows = pl.ds(start, SPAN)
            return pltpu.roll(jnp.where(lane < wrapped, ext_ref[after, rows, :], ext_ref[source, rows, :]), turn, 1)

        evens = jnp.where(first_even, window(0), window(2))
        odds = jnp.where(first_odd, window(1), window(3))
        total = None
        for tap in range(TAPS):
            value = jnp.where(even_group[tap], evens, odds)
            if tap:
                value = pltpu.roll(value, LANES - tap, 1)
            value = weights[TAPS + tap : TAPS + tap + 1] * value
            total = value if total is None else total + value
        pass_ref[slot] = total
        return weights

    def rows_of(device, tile_row, slot, weights):
        total = None
        for tap in range(TAPS):
            value = weights[tap : tap + 1] * pass_ref[slot, tap : tap + TILE, :]
            total = value if total is None else total + value
        phi_ref[device, tile_row * TILE : (tile_row + 1) * TILE, :] = total

    together = pass_ref.shape[0] // tile_rows

    def step(index, carry):
        work = []
        for place in range(together):
            device = index * together + place
            for tile_row in range(tile_rows):
                slot = place * tile_rows + tile_row
                work.append((device, tile_row, slot, columns(device, tile_row, slot)))
        for item in work:
            rows_of(*item)
        return carry

    lax.fori_loop(0, chunks // together, step, 0)
    for chunk in range(chunks):
        top_ref[2 * chunk : 2 * chunk + 2, :] = phi_ref[chunk, 0:2, :]
        bottom_ref[2 * chunk : 2 * chunk + 2, :] = phi_ref[chunk, cells - 2 : cells, :]


PAD = 8


def laplacian(ref, chunks, chunk, first, count):
    lane = lax.broadcasted_iota(jnp.int32, (count, LANES), 1)
    west = lax.rem(chunk + chunks - 1, chunks)
    east = lax.rem(chunk + 1, chunks)
    here = ref[chunk, first : first + count, :]
    from_west = pltpu.roll(jnp.where(lane == LANES - 1, ref[west, first : first + count, :], here), 1, 1)
    from_east = pltpu.roll(jnp.where(lane == 0, ref[east, first : first + count, :], here), LANES - 1, 1)
    beside = ref[chunk, first + 1 : first + 1 + count, :] + ref[chunk, first - 1 : first - 1 + count, :] + from_west + from_east
    return beside - 4.0 * here


def own_coef(coef_ref, half, chunks):
    levels = coef_ref.shape[1]
    member = half * chunks + lax.axis_index("lon")
    return coef_ref[member // levels, lax.rem(member, levels)]


def diffuse_kernel(half, coef_ref, phi_ref, psi_ref, lap_ref):
    chunks, cells = phi_ref.shape[0], phi_ref.shape[1]
    coef = own_coef(coef_ref, half, chunks)

    def first_pass(chunk, carry):
        lap_ref[chunk, PAD - 1 : cells - PAD + 1, :] = laplacian(phi_ref, chunks, chunk, PAD - 1, cells - 2 * PAD + 2)
        return carry

    def second_pass(chunk, carry):
        twice = laplacian(lap_ref, chunks, chunk, PAD, cells - 2 * PAD)
        psi_ref[chunk] = phi_ref[chunk, PAD : cells - PAD, :] - coef * twice
        return carry

    lax.fori_loop(0, chunks, first_pass, 0)
    lax.fori_loop(0, chunks, second_pass, 0)


def mend_kernel(half, coef_ref, phi_ref, north_ref, south_ref, inner_ref, psi_ref, ext_ref, lap_ref):
    chunks, cells = phi_ref.shape[0], phi_ref.shape[1]
    coef = own_coef(coef_ref, half, chunks)
    band = lax.axis_index("lat")
    has_north = jnp.where(band > 0, 1.0, 0.0)
    has_south = jnp.where(band < lax.axis_size("lat") - 1, 1.0, 0.0)
    zeros = jnp.zeros((PAD, LANES), jnp.float32)
    for chunk in range(chunks):
        place = chunk
        psi_ref[chunk, PAD : cells - PAD, :] = inner_ref[chunk]
        ext_ref[place, 0:PAD, :] = zeros
        ext_ref[place, 4 * PAD :, :] = zeros
        ext_ref[place, PAD : 2 * PAD, :] = zeros
        ext_ref[place, 2 * PAD - 2 : 2 * PAD, :] = north_ref[2 * chunk : 2 * chunk + 2, :]
        ext_ref[place, 2 * PAD : 4 * PAD, :] = phi_ref[chunk, 0 : 2 * PAD, :]
        place = chunks + chunk
        ext_ref[place, 0:PAD, :] = zeros
        ext_ref[place, 4 * PAD :, :] = zeros
        ext_ref[place, PAD : 3 * PAD, :] = phi_ref[chunk, cells - 2 * PAD :, :]
        ext_ref[place, 3 * PAD : 4 * PAD, :] = zeros
        ext_ref[place, 3 * PAD : 3 * PAD + 2, :] = south_ref[2 * chunk : 2 * chunk + 2, :]
    for side in range(2):
        own = pl.ds(side * chunks, chunks)
        for chunk in range(chunks):
            once = laplacian(ext_ref.at[own], chunks, chunk, PAD, 3 * PAD)
            place = side * chunks + chunk
            if side == 0:
                lap_ref[place, PAD : 2 * PAD, :] = once[0:PAD] * has_north
                lap_ref[place, 2 * PAD : 4 * PAD, :] = once[PAD:]
            else:
                lap_ref[place, PAD : 3 * PAD, :] = once[0 : 2 * PAD]
                lap_ref[place, 3 * PAD : 4 * PAD, :] = once[2 * PAD :] * has_south
    for side in range(2):
        own = pl.ds(side * chunks, chunks)
        rows = slice(0, PAD) if side == 0 else slice(cells - PAD, cells)
        for chunk in range(chunks):
            twice = laplacian(lap_ref.at[own], chunks, chunk, 2 * PAD, PAD)
            psi_ref[chunk, rows, :] = phi_ref[chunk, rows, :] - coef * twice


def vertical_kernel(levels, half, lower_ref, upper_ref, inverse_ref, psi_ref, *refs):
    out_ref = refs[-1]
    local = pl.program_id(0)
    field = half * pl.num_programs(0) + local
    sweep = []
    for level in range(levels):
        rhs = psi_ref[level]
        if level:
            rhs = rhs + lower_ref[field, level] * sweep[-1]
        sweep.append(rhs * inverse_ref[field, level])
    value = sweep[-1]
    out_ref[0, levels - 1] = value
    for level in range(levels - 2, -1, -1):
        value = sweep[level] - upper_ref[field, level] * value
        out_ref[0, level] = value


def vertical_tables(vert_coef):
    fcount = vert_coef.shape[0]
    levels = vert_coef.shape[1] + 1
    zero_column = jnp.zeros((fcount, 1), jnp.float32)
    lower_coef = jnp.concatenate([zero_column, vert_coef], axis=1)
    upper_coef = jnp.concatenate([vert_coef, zero_column], axis=1)
    diagonal = 1.0 + lower_coef + upper_coef
    uppers, inverses = [], []
    for level in range(levels):
        denominator = diagonal[:, level]
        if level:
            denominator = denominator + lower_coef[:, level] * uppers[-1]
        inverses.append(1.0 / denominator)
        uppers.append(-upper_coef[:, level] / denominator)
    return lower_coef, jnp.stack(uppers, axis=1), jnp.stack(inverses, axis=1)


SMEM = pltpu.MemorySpace.SMEM
VMEM = pltpu.MemorySpace.VMEM


def smem():
    return pl.BlockSpec(memory_space=SMEM)


def vmem():
    return pl.BlockSpec(memory_space=VMEM)


def anywhere():
    return pl.BlockSpec(memory_space=pl.ANY)


LIMIT = pltpu.CompilerParams(vmem_limit_bytes=48 * 1024 * 1024)


def along_lat(value, by):
    peers = lax.axis_size("lat")
    return lax.ppermute(value, "lat", [(i, i + by) for i in range(peers) if 0 <= i + by < peers])


def interpolated(places, info, blocks, north, south, cells):
    chunks, _, width = blocks.shape
    tile_rows = cells // TILE
    edge = jax.ShapeDtypeStruct((2 * chunks, width), jnp.float32)
    return pl.pallas_call(
        interpolate_kernel,
        out_shape=(jax.ShapeDtypeStruct((chunks, cells, width), jnp.float32), edge, edge),
        in_specs=[smem(), vmem(), vmem(), vmem(), vmem()],
        out_specs=(vmem(), vmem(), vmem()),
        scratch_shapes=[
            pltpu.VMEM((chunks, cells + 2 * TILE + 8, width), jnp.float32),
            pltpu.VMEM((2 * tile_rows, SPAN, width), jnp.float32),
            pltpu.SemaphoreType.DMA((3,)),
        ],
        compiler_params=LIMIT,
        name="interpolate",
    )(places, info, blocks, north, south)


def diffused(half, hyper_coef, phi):
    chunks, cells, width = phi.shape
    return pl.pallas_call(
        functools.partial(diffuse_kernel, half),
        out_shape=jax.ShapeDtypeStruct((chunks, cells - 2 * PAD, width), jnp.float32),
        in_specs=[smem(), vmem()],
        out_specs=vmem(),
        scratch_shapes=[pltpu.VMEM(phi.shape, jnp.float32)],
        compiler_params=LIMIT,
        name="diffuse",
    )(hyper_coef, phi)


def mended(half, hyper_coef, phi, above, below, inner):
    chunks, cells, width = phi.shape
    return pl.pallas_call(
        functools.partial(mend_kernel, half),
        out_shape=jax.ShapeDtypeStruct(phi.shape, jnp.float32),
        in_specs=[smem(), vmem(), vmem(), vmem(), vmem()],
        out_specs=vmem(),
        scratch_shapes=[
            pltpu.VMEM((2 * chunks, 5 * PAD, width), jnp.float32),
            pltpu.VMEM((2 * chunks, 5 * PAD, width), jnp.float32),
        ],
        compiler_params=LIMIT,
        name="mend",
    )(hyper_coef, phi, above, below, inner)


def solved(half, tables, psi, shape, earlier):
    fcount, levels, cells, width = shape
    part = fcount // HALVES
    operands = tables + (psi,) if earlier is None else tables + (psi, earlier)
    return pl.pallas_call(
        functools.partial(vertical_kernel, levels, half),
        grid=(part,),
        out_shape=jax.ShapeDtypeStruct(shape, jnp.float32),
        in_specs=[smem(), smem(), smem(), pl.BlockSpec((levels, cells, width), lambda field: (field, 0, 0))]
        + ([] if earlier is None else [anywhere()]),
        out_specs=pl.BlockSpec((1, levels, cells, width), lambda field: (half * part + field, 0, 0, 0)),
        input_output_aliases={} if earlier is None else {4: 0},
        compiler_params=LIMIT,
        name="solve",
    )(*operands)


def body(fields, hyper_coef, vert_coef, dep_owner, dep_row, dep_col, shifts, fracs):
    fcount, levels, cells, width = fields.shape
    chunks = lax.axis_size("lon")
    tile_rows = cells // TILE
    tile_cols = width // TILE
    tiles = tile_rows * tile_cols
    flat = fields.reshape(fcount * levels, cells, width)
    table = jnp.concatenate(
        [
            dep_owner.reshape(1, tiles),
            dep_row.reshape(1, tiles),
            dep_col.reshape(1, tiles),
            shifts.reshape(tiles, 2).T,
            fracs.reshape(tiles, 2).T,
        ],
        axis=0,
    )
    packed = pl.pallas_call(
        functools.partial(pack_kernel, tile_rows, tile_cols, lax.axis_size("lat") * tile_rows - 2),
        out_shape=jax.ShapeDtypeStruct((chunks, cells + INFO_ROWS, width), jnp.float32),
        in_specs=[anywhere(), vmem()],
        out_specs=vmem(),
        scratch_shapes=[pltpu.VMEM((8, LANES), jnp.int32), pltpu.SemaphoreType.DMA((1,))],
        compiler_params=LIMIT,
        name="pack",
    )(flat, table)
    blocks = [lax.all_to_all(packed, "lon", 0, 0, tiled=True), lax.all_to_all(flat[chunks:], "lon", 0, 0, tiled=True)]
    info = blocks[0]
    places = info[:, cells : cells + 4, tiles : 2 * tiles].astype(jnp.int32).reshape(chunks, 4 * tiles)
    tables = vertical_tables(vert_coef)
    out = None
    psis = []
    for half in range(HALVES):
        north = along_lat(blocks[half][:, cells - TILE : cells, :], 1)
        south = along_lat(blocks[half][:, :TILE, :], -1)
        phi, top, bottom = interpolated(places, info, blocks[half], north, south, cells)
        above = along_lat(bottom, 1)
        below = along_lat(top, -1)
        inner = diffused(half, hyper_coef, phi)
        psi = mended(half, hyper_coef, phi, above, below, inner)
        psis.append(lax.all_to_all(psi, "lon", 0, 0, tiled=True))
    for half in range(HALVES):
        out = solved(half, tables, psis[half], fields.shape, out)
    return out


def solution(mesh):
    cells = P(None, None, "lat", "lon")
    tiles = P("lat", "lon", None, None)
    return jax.shard_map(
        body,
        mesh=mesh,
        in_specs=(cells, P(), P(), tiles, tiles, tiles, tiles, tiles),
        out_specs=cells,
        check_vma=False,
    )
```

```python
import functools

import jax
import jax.numpy as jnp
import numpy as np
from jax import lax
from jax.experimental import pallas as pl
from jax.experimental.pallas import tpu as pltpu
from jax.sharding import Mesh, PartitionSpec as P

TILE = 32
FRACS = 16
LANES = 128
INFO_ROWS = 8
PAIR = 2
TAPS = 4
SPAN = 40


def cubic_weights(fraction_index):
    fraction = fraction_index.astype(jnp.float32) / FRACS
    return (
        -fraction * (fraction - 1.0) * (fraction - 2.0) / 6.0,
        (fraction + 1.0) * (fraction - 1.0) * (fraction - 2.0) / 2.0,
        -(fraction + 1.0) * fraction * (fraction - 2.0) / 2.0,
        (fraction + 1.0) * fraction * (fraction - 1.0) / 6.0,
    )


def swapped():
    return lax.rem(lax.axis_index("group"), 2)


def pack_kernel(tile_rows, tile_cols, last_row, fields_ref, table_ref, out_ref, wide_ref, sem):
    count, cells = fields_ref.shape[0], fields_ref.shape[1]
    half = count // PAIR
    swap = swapped()
    copies = []
    for part in range(PAIR):
        source = lax.bitwise_xor(part, swap) * half
        copies.append(
            pltpu.make_async_copy(
                fields_ref.at[pl.ds(source, half)], out_ref.at[part * half : (part + 1) * half, 0:cells, :], sem.at[part]
            )
        )
    for copy in copies:
        copy.start()
    entries, tiles = table_ref.shape
    group = lax.axis_index("group")
    band = group * PAIR + lax.axis_index("part")
    wide_ref[...] = jnp.zeros(wide_ref.shape, jnp.int32)
    wide_ref[0:entries, 0:tiles] = table_ref[...]
    table = wide_ref[...]
    owner, dep_row, dep_col = table[0:1], table[1:2], table[2:3]
    shift_row, shift_col, frac_row, frac_col = table[3:4], table[4:5], table[5:6], table[6:7]
    dep_tile = jnp.clip(band * tile_rows - 1 + dep_row, 0, last_row)
    start = TILE * (dep_tile - (group * PAIR * tile_rows - 1)) + shift_row - 1
    column = TILE * dep_col + shift_col - 1
    wrapped = jnp.where(dep_col == tile_cols - 1, TILE, 0)
    position = lax.rem(lax.broadcasted_iota(jnp.int32, (1, LANES), 1), tile_cols)
    turn = lax.bitwise_and(LANES + TILE * position - column, LANES - 1)
    shape = (INFO_ROWS, LANES)
    index = lax.broadcasted_iota(jnp.int32, shape, 0)
    lane = lax.broadcasted_iota(jnp.int32, shape, 1)
    info = jnp.zeros(shape, jnp.float32)
    for place, value in enumerate(cubic_weights(frac_row) + cubic_weights(frac_col)):
        info = jnp.where(index == place, value, info)
    places = jnp.zeros(shape, jnp.int32)
    for place, value in enumerate((start, owner, wrapped, turn)):
        places = jnp.where(index == place, value, places)
    info = jnp.where(lane < tiles, info, pltpu.roll(places.astype(jnp.float32), tiles, 1))
    for block in range(count):
        out_ref[block, cells:, :] = info
    for copy in copies:
        copy.wait()


def parts(value):
    high = value.astype(jnp.bfloat16)
    return high, (value - high.astype(jnp.float32)).astype(jnp.bfloat16)


def tap_matrix():
    matrix = np.zeros((2 * LANES, (TAPS - 1) * LANES), np.float32)
    for tap in range(1, TAPS):
        for lane in range(LANES):
            odd = (lane // TILE) % 2
            matrix[odd * LANES + (lane + tap) % LANES, (tap - 1) * LANES + lane] = 1.0
    return jnp.asarray(matrix, jnp.bfloat16)


def beside_matrix():
    matrix = np.zeros((3 * LANES, LANES), np.float32)
    for lane in range(LANES):
        matrix[LANES + lane - 1, lane] = 1.0
        matrix[LANES + lane + 1, lane] = 1.0
    return jnp.asarray(matrix, jnp.bfloat16)


PAD = 8


def interpolate_kernel(
    places_ref, blocks_ref, north_ref, south_ref, taps_ref, phi_ref, top_ref, bottom_ref, ext_ref, pass_ref, sem
):
    chunks, halo = north_ref.shape[0], north_ref.shape[1]
    rows = phi_ref.shape[1] - 2 * PAD
    cells = rows // PAIR
    tile_rows = cells // TILE
    tile_cols = LANES // TILE
    tiles = tile_rows * tile_cols
    copies = [
        pltpu.make_async_copy(north_ref, ext_ref.at[:, 0:halo, :], sem.at[0]),
        pltpu.make_async_copy(south_ref, ext_ref.at[:, halo + rows : 2 * halo + rows, :], sem.at[1]),
    ]
    for band in range(PAIR):
        copies.append(
            pltpu.make_async_copy(
                blocks_ref.at[band * chunks : (band + 1) * chunks, 0:cells, :],
                ext_ref.at[:, halo + band * cells : halo + (band + 1) * cells, :],
                sem.at[2 + band],
            )
        )
    for copy in copies:
        copy.start()
    for chunk in range(chunks):
        phi_ref[chunk, 0:PAD, :] = jnp.zeros((PAD, LANES), jnp.float32)
        phi_ref[chunk, PAD + rows :, :] = jnp.zeros((PAD, LANES), jnp.float32)
    for copy in copies:
        copy.wait()
    lane = lax.broadcasted_iota(jnp.int32, (SPAN, LANES), 1)
    lane_info = lax.broadcasted_iota(jnp.int32, (INFO_ROWS, LANES), 1)
    first_even = lane < 48
    first_odd = (lane >= 16) & (lane < 80)
    even_group = lax.bitwise_and(lane, TILE) == 0
    together = pass_ref.shape[0] // tile_rows

    def windows(device, tile_row):
        def window(tile_col):
            tile = tile_row * tile_cols + tile_col
            start, source, wrapped, turn = (places_ref[device, place * tiles + tile] for place in range(4))
            after = lax.rem(source + 1, chunks)
            span = pl.ds(start, SPAN)
            return pltpu.roll(jnp.where(lane < wrapped, ext_ref[after, span, :], ext_ref[source, span, :]), turn, 1)

        return jnp.where(first_even, window(0), window(2)), jnp.where(first_odd, window(1), window(3))

    def step(index, carry):
        work = [(index * together + place, tile_row) for place in range(together) for tile_row in range(tile_rows)]
        pairs = [windows(*item) for item in work]
        evens = jnp.concatenate([pair[0] for pair in pairs], axis=0)
        odds = jnp.concatenate([pair[1] for pair in pairs], axis=0)
        even_parts, odd_parts = parts(evens), parts(odds)
        moved = None
        for which in range(2):
            part = jnp.dot(
                jnp.concatenate([even_parts[which], odd_parts[which]], axis=1),
                taps_ref[...],
                preferred_element_type=jnp.float32,
            )
            moved = part if moved is None else moved + part
        for slot, (device, tile_row) in enumerate(work):
            own = lane_info // TILE + tile_row * tile_cols
            weights = jnp.take_along_axis(blocks_ref[device, cells:, :], own, axis=1)
            total = weights[TAPS : TAPS + 1] * jnp.where(even_group, *pairs[slot])
            here = slice(slot * SPAN, (slot + 1) * SPAN)
            for tap in range(1, TAPS):
                total = total + weights[TAPS + tap : TAPS + tap + 1] * moved[here, (tap - 1) * LANES : tap * LANES]
            pass_ref[slot] = total
            total = None
            for tap in range(TAPS):
                value = weights[tap : tap + 1] * pass_ref[slot, tap : tap + TILE, :]
                total = value if total is None else total + value
            first = pl.multiple_of(PAD + (device // chunks) * cells + tile_row * TILE, PAD)
            phi_ref[lax.rem(device, chunks), pl.ds(first, TILE), :] = total
        return carry

    lax.fori_loop(0, PAIR * chunks // together, step, 0)
    for row in range(2):
        for chunk in range(chunks):
            place = row * chunks + chunk
            top_ref[place : place + 1, :] = phi_ref[chunk, PAD + row : PAD + row + 1, :]
            bottom_ref[place : place + 1, :] = phi_ref[chunk, PAD + rows - 2 + row : PAD + rows - 1 + row, :]


def own_coef(coef_ref, half):
    levels = coef_ref.shape[1]
    member = lax.bitwise_xor(lax.axis_index("part"), swapped()) * half + lax.axis_index("lon")
    return coef_ref[member // levels, lax.rem(member, levels)]


TOGETHER = 4


def diffuse_kernel(groups, coef_ref, phi_ref, beside_ref, psi_ref, lap_ref, high_ref, low_ref):
    chunks, rows = phi_ref.shape[0], phi_ref.shape[1] - 2 * PAD
    cells = rows // PAIR
    coef = own_coef(coef_ref, chunks)
    group = lax.axis_index("group")
    has_north = jnp.where(group > 0, 1.0, 0.0)
    has_south = jnp.where(group < groups - 1, 1.0, 0.0)
    together = min(TOGETHER, chunks)

    def laplacian(ref, store):
        for chunk in range(chunks):
            high, low = parts(ref[chunk, PAD : PAD + rows, :])
            high_ref[chunk], low_ref[chunk] = high, low

        def step(index, carry):
            members = [index * together + place for place in range(together)]
            sums = None
            for part_ref in (high_ref, low_ref):
                left = [
                    jnp.concatenate([part_ref[lax.rem(chunk + chunks + by, chunks)] for chunk in members], axis=0)
                    for by in (-1, 0, 1)
                ]
                part = jnp.dot(jnp.concatenate(left, axis=1), beside_ref[...], preferred_element_type=jnp.float32)
                sums = part if sums is None else sums + part
            for place, chunk in enumerate(members):
                around = ref[chunk, PAD + 1 : PAD + 1 + rows, :] + ref[chunk, PAD - 1 : PAD - 1 + rows, :]
                store(chunk, around + sums[place * rows : (place + 1) * rows] - 4.0 * ref[chunk, PAD : PAD + rows, :])
            return carry

        lax.fori_loop(0, chunks // together, step, 0)

    def keep(chunk, value):
        lap_ref[chunk, PAD : PAD + rows, :] = value
        lap_ref[chunk, PAD - 1 : PAD, :] = phi_ref[chunk, PAD : PAD + 1, :] * has_north
        lap_ref[chunk, PAD + rows : PAD + rows + 1, :] = phi_ref[chunk, PAD + rows - 1 : PAD + rows, :] * has_south

    def finish(chunk, value):
        psi = phi_ref[chunk, PAD : PAD + rows, :] - coef * value
        for band in range(PAIR):
            psi_ref[band * chunks + chunk] = psi[band * cells : (band + 1) * cells]

    laplacian(phi_ref, keep)
    laplacian(lap_ref, finish)


def mend_kernel(coef_ref, north_ref, south_ref, inner_ref, psi_ref):
    count, cells = psi_ref.shape[0], psi_ref.shape[1]
    chunks = count // PAIR
    coef = own_coef(coef_ref, chunks)
    shape = (chunks, LANES)
    lane = lax.broadcasted_iota(jnp.int32, shape, 1)

    def near_far(near, far):
        west = pltpu.roll(jnp.where(lane == LANES - 1, pltpu.roll(near, 1, 0), near), 1, 1)
        east = pltpu.roll(jnp.where(lane == 0, pltpu.roll(near, chunks - 1, 0), near), LANES - 1, 1)
        return coef * (far + 2.0 * (west + east) - 8.0 * near), coef * near

    psi_ref[...] = inner_ref[...]
    north = near_far(north_ref[chunks:, :], north_ref[0:chunks, :])
    south = near_far(south_ref[0:chunks, :], south_ref[chunks:, :])
    for chunk in range(chunks):
        low = chunk + (PAIR - 1) * chunks
        for row in range(2):
            here = slice(row, row + 1)
            psi_ref[chunk, here, :] = inner_ref[chunk, here, :] - north[row][chunk : chunk + 1]
            here = slice(cells - 1 - row, cells - row)
            psi_ref[low, here, :] = inner_ref[low, here, :] - south[row][chunk : chunk + 1]


def vertical_kernel(levels, lower_ref, upper_ref, inverse_ref, psi_ref, out_ref):
    field = pl.program_id(0)
    source = lax.bitwise_xor(field, swapped() * (pl.num_programs(0) // PAIR)) * levels
    step = 16
    for first in range(0, psi_ref.shape[1], step):
        rows = slice(first, first + step)
        sweep = []
        for level in range(levels):
            rhs = psi_ref[source + level, rows, :]
            if level:
                rhs = rhs + lower_ref[field, level] * sweep[-1]
            sweep.append(rhs * inverse_ref[field, level])
        value = sweep[-1]
        out_ref[0, levels - 1, rows, :] = value
        for level in range(levels - 2, -1, -1):
            value = sweep[level] - upper_ref[field, level] * value
            out_ref[0, level, rows, :] = value


def vertical_tables(vert_coef):
    fcount = vert_coef.shape[0]
    levels = vert_coef.shape[1] + 1
    zero_column = jnp.zeros((fcount, 1), jnp.float32)
    lower_coef = jnp.concatenate([zero_column, vert_coef], axis=1)
    upper_coef = jnp.concatenate([vert_coef, zero_column], axis=1)
    diagonal = 1.0 + lower_coef + upper_coef
    uppers, inverses = [], []
    for level in range(levels):
        denominator = diagonal[:, level]
        if level:
            denominator = denominator + lower_coef[:, level] * uppers[-1]
        inverses.append(1.0 / denominator)
        uppers.append(-upper_coef[:, level] / denominator)
    return lower_coef, jnp.stack(uppers, axis=1), jnp.stack(inverses, axis=1)


SMEM = pltpu.MemorySpace.SMEM
VMEM = pltpu.MemorySpace.VMEM


def smem():
    return pl.BlockSpec(memory_space=SMEM)


def vmem():
    return pl.BlockSpec(memory_space=VMEM)


def anywhere():
    return pl.BlockSpec(memory_space=pl.ANY)


def body(fields, hyper_coef, vert_coef, dep_owner, dep_row, dep_col, shifts, fracs):
    fcount, levels, cells, width = fields.shape
    count = fcount * levels
    chunks = lax.axis_size("lon")
    groups = lax.axis_size("group")
    tile_rows = cells // TILE
    tile_cols = width // TILE
    tiles = tile_rows * tile_cols
    rows = PAIR * cells
    f32 = jnp.float32
    limit = pltpu.CompilerParams(vmem_limit_bytes=48 * 1024 * 1024)

    table = jnp.concatenate(
        [
            dep_owner.reshape(1, tiles),
            dep_row.reshape(1, tiles),
            dep_col.reshape(1, tiles),
            shifts.reshape(tiles, 2).T,
            fracs.reshape(tiles, 2).T,
        ],
        axis=0,
    )
    blocks = pl.pallas_call(
        functools.partial(pack_kernel, tile_rows, tile_cols, groups * PAIR * tile_rows - 2),
        out_shape=jax.ShapeDtypeStruct((count, cells + INFO_ROWS, width), f32),
        in_specs=[anywhere(), vmem()],
        out_specs=vmem(),
        scratch_shapes=[pltpu.VMEM((8, LANES), jnp.int32), pltpu.SemaphoreType.DMA((PAIR,))],
        compiler_params=limit,
        name="pack",
    )(fields.reshape(count, cells, width), table)
    blocks = lax.all_to_all(blocks, ("part", "lon"), 0, 0, tiled=True)
    southward = [
        (group * PAIR + part, (group + 1) * PAIR + PAIR - 1 - part) for group in range(groups - 1) for part in range(PAIR)
    ]
    northward = [(target, source) for source, target in southward]
    bands = ("group", "part")
    north = lax.ppermute(blocks[(PAIR - 1) * chunks :, cells - TILE : cells, :], bands, southward)
    south = lax.ppermute(blocks[:chunks, :TILE, :], bands, northward)
    places = blocks[:, cells : cells + 4, tiles : 2 * tiles].astype(jnp.int32).reshape(PAIR * chunks, 4 * tiles)
    edge = jax.ShapeDtypeStruct((2 * chunks, width), f32)
    phi, top, bottom = pl.pallas_call(
        interpolate_kernel,
        out_shape=(jax.ShapeDtypeStruct((chunks, rows + 2 * PAD, width), f32), edge, edge),
        in_specs=[smem(), vmem(), vmem(), vmem(), vmem()],
        out_specs=(vmem(), vmem(), vmem()),
        scratch_shapes=[
            pltpu.VMEM((chunks, rows + 2 * TILE + 8, width), f32),
            pltpu.VMEM((min(8, chunks) * tile_rows, SPAN, width), f32),
            pltpu.SemaphoreType.DMA((2 + PAIR,)),
        ],
        compiler_params=limit,
        name="interpolate",
    )(places, blocks, north, south, tap_matrix())
    above = lax.ppermute(bottom, bands, southward)
    below = lax.ppermute(top, bands, northward)
    psi_shape = jax.ShapeDtypeStruct((count, cells, width), f32)
    inner = pl.pallas_call(
        functools.partial(diffuse_kernel, groups),
        out_shape=psi_shape,
        in_specs=[smem(), vmem(), vmem()],
        out_specs=vmem(),
        scratch_shapes=[
            pltpu.VMEM((chunks, rows + 2 * PAD, width), f32),
            pltpu.VMEM((chunks, rows, width), jnp.bfloat16),
            pltpu.VMEM((chunks, rows, width), jnp.bfloat16),
        ],
        compiler_params=limit,
        name="diffuse",
    )(hyper_coef, phi, beside_matrix())
    psi = pl.pallas_call(
        mend_kernel,
        out_shape=psi_shape,
        in_specs=[smem(), vmem(), vmem(), vmem()],
        out_specs=vmem(),
        compiler_params=limit,
        name="mend",
    )(hyper_coef, above, below, inner)
    psi = lax.all_to_all(psi, ("part", "lon"), 0, 0, tiled=True)
    lower, upper, inverse = vertical_tables(vert_coef)
    return pl.pallas_call(
        functools.partial(vertical_kernel, levels),
        grid=(fcount,),
        out_shape=jax.ShapeDtypeStruct((fcount, levels, cells, width), f32),
        in_specs=[smem(), smem(), smem(), vmem()],
        out_specs=pl.BlockSpec((1, levels, cells, width), lambda field: (field, 0, 0, 0)),
        compiler_params=limit,
    )(lower, upper, inverse, psi)


def solution(mesh):
    lat, lon = mesh.shape["lat"], mesh.shape["lon"]
    grouped = Mesh(mesh.devices.reshape(lat // PAIR, PAIR, lon), ("group", "part", "lon"))
    bands = ("group", "part")
    cells = P(None, None, bands, "lon")
    tiles = P(bands, "lon", None, None)
    return jax.shard_map(
        body,
        mesh=grouped,
        in_specs=(cells, P(), P(), tiles, tiles, tiles, tiles, tiles),
        out_specs=cells,
        check_vma=False,
    )
```

```python
import functools

import jax
import jax.numpy as jnp
import numpy as np
from jax import lax
from jax.experimental import pallas as pl
from jax.experimental.pallas import tpu as pltpu
from jax.sharding import Mesh, PartitionSpec as P

TILE = 32
FRACS = 16
LANES = 128
INFO_ROWS = 8
PAIR = 2
TAPS = 4
SPAN = 40


def cubic_weights(fraction_index):
    fraction = fraction_index.astype(jnp.float32) / FRACS
    return (
        -fraction * (fraction - 1.0) * (fraction - 2.0) / 6.0,
        (fraction + 1.0) * (fraction - 1.0) * (fraction - 2.0) / 2.0,
        -(fraction + 1.0) * fraction * (fraction - 2.0) / 2.0,
        (fraction + 1.0) * fraction * (fraction - 1.0) / 6.0,
    )


def swapped():
    return lax.rem(lax.axis_index("group"), 2)


def pack_kernel(tile_rows, tile_cols, last_row, fields_ref, table_ref, out_ref, wide_ref, sem):
    count, cells = fields_ref.shape[0], fields_ref.shape[1]
    half = count // PAIR
    swap = swapped()
    copies = []
    for part in range(PAIR):
        source = lax.bitwise_xor(part, swap) * half
        copies.append(
            pltpu.make_async_copy(
                fields_ref.at[pl.ds(source, half)], out_ref.at[part * half : (part + 1) * half, 0:cells, :], sem.at[part]
            )
        )
    for copy in copies:
        copy.start()
    entries, tiles = table_ref.shape
    group = lax.axis_index("group")
    band = group * PAIR + lax.axis_index("part")
    wide_ref[...] = jnp.zeros(wide_ref.shape, jnp.int32)
    wide_ref[0:entries, 0:tiles] = table_ref[...]
    table = wide_ref[...]
    owner, dep_row, dep_col = table[0:1], table[1:2], table[2:3]
    shift_row, shift_col, frac_row, frac_col = table[3:4], table[4:5], table[5:6], table[6:7]
    dep_tile = jnp.clip(band * tile_rows - 1 + dep_row, 0, last_row)
    start = TILE * (dep_tile - (group * PAIR * tile_rows - 1)) + shift_row - 1
    column = TILE * dep_col + shift_col - 1
    wrapped = jnp.where(dep_col == tile_cols - 1, TILE, 0)
    position = lax.rem(lax.broadcasted_iota(jnp.int32, (1, LANES), 1), tile_cols)
    turn = lax.bitwise_and(LANES + TILE * position - column, LANES - 1)
    shape = (INFO_ROWS, LANES)
    index = lax.broadcasted_iota(jnp.int32, shape, 0)
    lane = lax.broadcasted_iota(jnp.int32, shape, 1)
    info = jnp.zeros(shape, jnp.float32)
    for place, value in enumerate(cubic_weights(frac_row) + cubic_weights(frac_col)):
        info = jnp.where(index == place, value, info)
    places = jnp.zeros(shape, jnp.int32)
    for place, value in enumerate((start, owner, wrapped, turn)):
        places = jnp.where(index == place, value, places)
    info = jnp.where(lane < tiles, info, pltpu.roll(places.astype(jnp.float32), tiles, 1))
    for block in range(count):
        out_ref[block, cells:, :] = info
    for copy in copies:
        copy.wait()


def parts(value):
    high = value.astype(jnp.bfloat16)
    return high, (value - high.astype(jnp.float32)).astype(jnp.bfloat16)


def tap_matrix():
    matrix = np.zeros((2 * LANES, (TAPS - 1) * LANES), np.float32)
    for tap in range(1, TAPS):
        for lane in range(LANES):
            odd = (lane // TILE) % 2
            matrix[odd * LANES + (lane + tap) % LANES, (tap - 1) * LANES + lane] = 1.0
    return jnp.asarray(matrix, jnp.bfloat16)


def beside_matrix():
    matrix = np.zeros((3 * LANES, LANES), np.float32)
    for lane in range(LANES):
        matrix[LANES + lane - 1, lane] = 1.0
        matrix[LANES + lane + 1, lane] = 1.0
    return jnp.asarray(matrix, jnp.bfloat16)


PAD = 8


def interpolate_kernel(
    places_ref, blocks_ref, north_ref, south_ref, taps_ref, phi_ref, top_ref, bottom_ref, ext_ref, pass_ref, sem
):
    chunks, halo = north_ref.shape[0], north_ref.shape[1]
    rows = phi_ref.shape[1] - 2 * PAD
    cells = rows // PAIR
    tile_rows = cells // TILE
    tile_cols = LANES // TILE
    tiles = tile_rows * tile_cols
    copies = [
        pltpu.make_async_copy(north_ref, ext_ref.at[:, 0:halo, :], sem.at[0]),
        pltpu.make_async_copy(south_ref, ext_ref.at[:, halo + rows : 2 * halo + rows, :], sem.at[1]),
    ]
    for band in range(PAIR):
        copies.append(
            pltpu.make_async_copy(
                blocks_ref.at[band * chunks : (band + 1) * chunks, 0:cells, :],
                ext_ref.at[:, halo + band * cells : halo + (band + 1) * cells, :],
                sem.at[2 + band],
            )
        )
    for copy in copies:
        copy.start()
    for chunk in range(chunks):
        phi_ref[chunk, 0:PAD, :] = jnp.zeros((PAD, LANES), jnp.float32)
        phi_ref[chunk, PAD + rows :, :] = jnp.zeros((PAD, LANES), jnp.float32)
    for copy in copies:
        copy.wait()
    lane = lax.broadcasted_iota(jnp.int32, (SPAN, LANES), 1)
    lane_info = lax.broadcasted_iota(jnp.int32, (INFO_ROWS, LANES), 1)
    first_even = lane < 48
    first_odd = (lane >= 16) & (lane < 80)
    even_group = lax.bitwise_and(lane, TILE) == 0
    together = pass_ref.shape[0] // tile_rows

    def windows(device, tile_row):
        def window(tile_col):
            tile = tile_row * tile_cols + tile_col
            start, source, wrapped, turn = (places_ref[device, place * tiles + tile] for place in range(4))
            after = lax.rem(source + 1, chunks)
            span = pl.ds(start, SPAN)
            return pltpu.roll(jnp.where(lane < wrapped, ext_ref[after, span, :], ext_ref[source, span, :]), turn, 1)

        return jnp.where(first_even, window(0), window(2)), jnp.where(first_odd, window(1), window(3))

    def step(index, carry):
        work = [(index * together + place, tile_row) for place in range(together) for tile_row in range(tile_rows)]
        pairs = [windows(*item) for item in work]
        evens = jnp.concatenate([pair[0] for pair in pairs], axis=0)
        odds = jnp.concatenate([pair[1] for pair in pairs], axis=0)
        even_parts, odd_parts = parts(evens), parts(odds)
        moved = None
        for which in range(2):
            part = jnp.dot(
                jnp.concatenate([even_parts[which], odd_parts[which]], axis=1),
                taps_ref[...],
                preferred_element_type=jnp.float32,
            )
            moved = part if moved is None else moved + part
        for slot, (device, tile_row) in enumerate(work):
            own = lane_info // TILE + tile_row * tile_cols
            weights = jnp.take_along_axis(blocks_ref[device, cells:, :], own, axis=1)
            total = weights[TAPS : TAPS + 1] * jnp.where(even_group, *pairs[slot])
            here = slice(slot * SPAN, (slot + 1) * SPAN)
            for tap in range(1, TAPS):
                total = total + weights[TAPS + tap : TAPS + tap + 1] * moved[here, (tap - 1) * LANES : tap * LANES]
            pass_ref[slot] = total
            total = None
            for tap in range(TAPS):
                value = weights[tap : tap + 1] * pass_ref[slot, tap : tap + TILE, :]
                total = value if total is None else total + value
            first = pl.multiple_of(PAD + (device // chunks) * cells + tile_row * TILE, PAD)
            phi_ref[lax.rem(device, chunks), pl.ds(first, TILE), :] = total
        return carry

    lax.fori_loop(0, PAIR * chunks // together, step, 0)
    for row in range(2):
        for chunk in range(chunks):
            place = row * chunks + chunk
            top_ref[place : place + 1, :] = phi_ref[chunk, PAD + row : PAD + row + 1, :]
            bottom_ref[place : place + 1, :] = phi_ref[chunk, PAD + rows - 2 + row : PAD + rows - 1 + row, :]


def own_coef(coef_ref, half):
    levels = coef_ref.shape[1]
    member = lax.bitwise_xor(lax.axis_index("part"), swapped()) * half + lax.axis_index("lon")
    return coef_ref[member // levels, lax.rem(member, levels)]


TOGETHER = 4


def diffuse_kernel(groups, coef_ref, phi_ref, beside_ref, psi_ref, lap_ref, high_ref, low_ref):
    chunks, rows = phi_ref.shape[0], phi_ref.shape[1] - 2 * PAD
    cells = rows // PAIR
    coef = own_coef(coef_ref, chunks)
    group = lax.axis_index("group")
    has_north = jnp.where(group > 0, 1.0, 0.0)
    has_south = jnp.where(group < groups - 1, 1.0, 0.0)
    together = min(TOGETHER, chunks)

    def laplacian(ref, store):
        for chunk in range(chunks):
            high, low = parts(ref[chunk, PAD : PAD + rows, :])
            high_ref[chunk], low_ref[chunk] = high, low

        def step(index, carry):
            members = [index * together + place for place in range(together)]
            sums = None
            for part_ref in (high_ref, low_ref):
                left = [
                    jnp.concatenate([part_ref[lax.rem(chunk + chunks + by, chunks)] for chunk in members], axis=0)
                    for by in (-1, 0, 1)
                ]
                part = jnp.dot(jnp.concatenate(left, axis=1), beside_ref[...], preferred_element_type=jnp.float32)
                sums = part if sums is None else sums + part
            for place, chunk in enumerate(members):
                around = ref[chunk, PAD + 1 : PAD + 1 + rows, :] + ref[chunk, PAD - 1 : PAD - 1 + rows, :]
                store(chunk, around + sums[place * rows : (place + 1) * rows] - 4.0 * ref[chunk, PAD : PAD + rows, :])
            return carry

        lax.fori_loop(0, chunks // together, step, 0)

    def keep(chunk, value):
        lap_ref[chunk, PAD : PAD + rows, :] = value
        lap_ref[chunk, PAD - 1 : PAD, :] = phi_ref[chunk, PAD : PAD + 1, :] * has_north
        lap_ref[chunk, PAD + rows : PAD + rows + 1, :] = phi_ref[chunk, PAD + rows - 1 : PAD + rows, :] * has_south

    def finish(chunk, value):
        psi = phi_ref[chunk, PAD : PAD + rows, :] - coef * value
        for band in range(PAIR):
            psi_ref[band * chunks + chunk] = psi[band * cells : (band + 1) * cells]

    laplacian(phi_ref, keep)
    laplacian(lap_ref, finish)


def mend_kernel(groups, coef_ref, north_ref, south_ref, inner_ref, psi_ref):
    count, cells = psi_ref.shape[0], psi_ref.shape[1]
    chunks = count // PAIR
    coef = own_coef(coef_ref, chunks)
    shape = (chunks, LANES)
    lane = lax.broadcasted_iota(jnp.int32, shape, 1)

    group = lax.axis_index("group")
    has_north = jnp.where(group > 0, 1.0, 0.0)
    has_south = jnp.where(group < groups - 1, 1.0, 0.0)

    def near_far(near, far, coef):
        west = pltpu.roll(jnp.where(lane == LANES - 1, pltpu.roll(near, 1, 0), near), 1, 1)
        east = pltpu.roll(jnp.where(lane == 0, pltpu.roll(near, chunks - 1, 0), near), LANES - 1, 1)
        return coef * (far + 2.0 * (west + east) - 8.0 * near), coef * near

    psi_ref[...] = inner_ref[...]
    north = near_far(north_ref[chunks:, :], north_ref[0:chunks, :], coef * has_north)
    south = near_far(south_ref[0:chunks, :], south_ref[chunks:, :], coef * has_south)
    for chunk in range(chunks):
        low = chunk + (PAIR - 1) * chunks
        for row in range(2):
            here = slice(row, row + 1)
            psi_ref[chunk, here, :] = inner_ref[chunk, here, :] - north[row][chunk : chunk + 1]
            here = slice(cells - 1 - row, cells - row)
            psi_ref[low, here, :] = inner_ref[low, here, :] - south[row][chunk : chunk + 1]


def vertical_kernel(lower_ref, upper_ref, inverse_ref, psi_ref, out_ref, held_ref, sem):
    fcount, levels, cells, _ = held_ref.shape
    step = 16
    copies = []
    swap = swapped()
    for field in range(fcount):
        source = lax.bitwise_xor(field, swap * (fcount // PAIR)) * levels
        for first in range(0, cells, step):
            rows = slice(first, first + step)
            sweep = []
            for level in range(levels):
                rhs = psi_ref[source + level, rows, :]
                if level:
                    rhs = rhs + lower_ref[field, level] * sweep[-1]
                sweep.append(rhs * inverse_ref[field, level])
            value = sweep[-1]
            held_ref[field, levels - 1, rows, :] = value
            for level in range(levels - 2, -1, -1):
                value = sweep[level] - upper_ref[field, level] * value
                held_ref[field, level, rows, :] = value
        copy = pltpu.make_async_copy(held_ref.at[field], out_ref.at[field], sem.at[field])
        copy.start()
        copies.append(copy)
    for copy in copies:
        copy.wait()


def vertical_tables(vert_coef):
    fcount = vert_coef.shape[0]
    levels = vert_coef.shape[1] + 1
    zero_column = jnp.zeros((fcount, 1), jnp.float32)
    lower_coef = jnp.concatenate([zero_column, vert_coef], axis=1)
    upper_coef = jnp.concatenate([vert_coef, zero_column], axis=1)
    diagonal = 1.0 + lower_coef + upper_coef
    uppers, inverses = [], []
    for level in range(levels):
        denominator = diagonal[:, level]
        if level:
            denominator = denominator + lower_coef[:, level] * uppers[-1]
        inverses.append(1.0 / denominator)
        uppers.append(-upper_coef[:, level] / denominator)
    return lower_coef, jnp.stack(uppers, axis=1), jnp.stack(inverses, axis=1)


SMEM = pltpu.MemorySpace.SMEM
VMEM = pltpu.MemorySpace.VMEM


def smem():
    return pl.BlockSpec(memory_space=SMEM)


def vmem():
    return pl.BlockSpec(memory_space=VMEM)


def anywhere():
    return pl.BlockSpec(memory_space=pl.ANY)


def body(fields, hyper_coef, vert_coef, dep_owner, dep_row, dep_col, shifts, fracs):
    fcount, levels, cells, width = fields.shape
    count = fcount * levels
    chunks = lax.axis_size("lon")
    groups = lax.axis_size("group")
    tile_rows = cells // TILE
    tile_cols = width // TILE
    tiles = tile_rows * tile_cols
    rows = PAIR * cells
    f32 = jnp.float32
    limit = pltpu.CompilerParams(vmem_limit_bytes=48 * 1024 * 1024)

    table = jnp.concatenate(
        [
            dep_owner.reshape(1, tiles),
            dep_row.reshape(1, tiles),
            dep_col.reshape(1, tiles),
            shifts.reshape(tiles, 2).T,
            fracs.reshape(tiles, 2).T,
        ],
        axis=0,
    )
    blocks = pl.pallas_call(
        functools.partial(pack_kernel, tile_rows, tile_cols, groups * PAIR * tile_rows - 2),
        out_shape=jax.ShapeDtypeStruct((count, cells + INFO_ROWS, width), f32),
        in_specs=[anywhere(), vmem()],
        out_specs=vmem(),
        scratch_shapes=[pltpu.VMEM((8, LANES), jnp.int32), pltpu.SemaphoreType.DMA((PAIR,))],
        compiler_params=limit,
        name="pack",
    )(fields.reshape(count, cells, width), table)
    blocks = lax.all_to_all(blocks, ("part", "lon"), 0, 0, tiled=True)
    southward = [
        (group * PAIR + part, (group + 1) % groups * PAIR + PAIR - 1 - part) for group in range(groups) for part in range(PAIR)
    ]
    northward = [(target, source) for source, target in southward]
    bands = ("group", "part")
    north = lax.ppermute(blocks[(PAIR - 1) * chunks :, cells - TILE : cells, :], bands, southward)
    south = lax.ppermute(blocks[:chunks, :TILE, :], bands, northward)
    places = blocks[:, cells : cells + 4, tiles : 2 * tiles].astype(jnp.int32).reshape(PAIR * chunks, 4 * tiles)
    edge = jax.ShapeDtypeStruct((2 * chunks, width), f32)
    phi, top, bottom = pl.pallas_call(
        interpolate_kernel,
        out_shape=(jax.ShapeDtypeStruct((chunks, rows + 2 * PAD, width), f32), edge, edge),
        in_specs=[smem(), vmem(), vmem(), vmem(), vmem()],
        out_specs=(vmem(), vmem(), vmem()),
        scratch_shapes=[
            pltpu.VMEM((chunks, rows + 2 * TILE + 8, width), f32),
            pltpu.VMEM((min(8, chunks) * tile_rows, SPAN, width), f32),
            pltpu.SemaphoreType.DMA((2 + PAIR,)),
        ],
        compiler_params=limit,
        name="interpolate",
    )(places, blocks, north, south, tap_matrix())
    above = lax.ppermute(bottom, bands, southward)
    below = lax.ppermute(top, bands, northward)
    psi_shape = jax.ShapeDtypeStruct((count, cells, width), f32)
    inner = pl.pallas_call(
        functools.partial(diffuse_kernel, groups),
        out_shape=psi_shape,
        in_specs=[smem(), vmem(), vmem()],
        out_specs=vmem(),
        scratch_shapes=[
            pltpu.VMEM((chunks, rows + 2 * PAD, width), f32),
            pltpu.VMEM((chunks, rows, width), jnp.bfloat16),
            pltpu.VMEM((chunks, rows, width), jnp.bfloat16),
        ],
        compiler_params=limit,
        name="diffuse",
    )(hyper_coef, phi, beside_matrix())
    psi = pl.pallas_call(
        functools.partial(mend_kernel, groups),
        out_shape=psi_shape,
        in_specs=[smem(), vmem(), vmem(), vmem()],
        out_specs=vmem(),
        compiler_params=limit,
        name="mend",
    )(hyper_coef, above, below, inner)
    psi = lax.all_to_all(psi, ("part", "lon"), 0, 0, tiled=True)
    lower, upper, inverse = vertical_tables(vert_coef)
    return pl.pallas_call(
        vertical_kernel,
        out_shape=jax.ShapeDtypeStruct((fcount, levels, cells, width), f32),
        in_specs=[smem(), smem(), smem(), vmem()],
        out_specs=anywhere(),
        scratch_shapes=[pltpu.VMEM((fcount, levels, cells, width), f32), pltpu.SemaphoreType.DMA((fcount,))],
        compiler_params=limit,
        name="solve",
    )(lower, upper, inverse, psi)


def solution(mesh):
    lat, lon = mesh.shape["lat"], mesh.shape["lon"]
    grouped = Mesh(mesh.devices.reshape(lat // PAIR, PAIR, lon), ("group", "part", "lon"))
    bands = ("group", "part")
    cells = P(None, None, bands, "lon")
    tiles = P(bands, "lon", None, None)
    return jax.shard_map(
        body,
        mesh=grouped,
        in_specs=(cells, P(), P(), tiles, tiles, tiles, tiles, tiles),
        out_specs=cells,
        check_vma=False,
    )
```

```python
import functools

import jax
import jax.numpy as jnp
import numpy as np
from jax import lax
from jax.experimental import pallas as pl
from jax.experimental.pallas import tpu as pltpu
from jax.sharding import Mesh, PartitionSpec as P

TILE = 32
FRACS = 16
LANES = 128
INFO_ROWS = 8
PAIR = 2
TAPS = 4
SPAN = 40


def cubic_weights(fraction_index):
    fraction = fraction_index.astype(jnp.float32) / FRACS
    return (
        -fraction * (fraction - 1.0) * (fraction - 2.0) / 6.0,
        (fraction + 1.0) * (fraction - 1.0) * (fraction - 2.0) / 2.0,
        -(fraction + 1.0) * fraction * (fraction - 2.0) / 2.0,
        (fraction + 1.0) * fraction * (fraction - 1.0) / 6.0,
    )


def swapped():
    return lax.rem(lax.axis_index("group"), 2)


def pack_kernel(tile_rows, tile_cols, last_row, fields_ref, table_ref, out_ref, rest_ref, wide_ref, sem):
    count = fields_ref.shape[0]
    half = count // PAIR
    swap = swapped()
    group = lax.axis_index("group")
    part = lax.axis_index("part")
    border = pl.ds(pl.multiple_of(part * TILE, TILE), TILE)
    inner = pl.ds(pl.multiple_of((1 - part) * TILE, TILE), TILE)
    copies = []
    for place in range(PAIR):
        source = pl.ds(lax.bitwise_xor(place, swap) * half, half)
        blocks = slice(place * half, (place + 1) * half)
        copies.append(pltpu.make_async_copy(fields_ref.at[source, border], out_ref.at[blocks, 0:TILE, :], sem.at[2 * place]))
        copies.append(pltpu.make_async_copy(fields_ref.at[source, inner], rest_ref.at[blocks], sem.at[2 * place + 1]))
    for copy in copies:
        copy.start()
    entries, tiles = table_ref.shape
    band = group * PAIR + part
    wide_ref[...] = jnp.zeros(wide_ref.shape, jnp.int32)
    wide_ref[0:entries, 0:tiles] = table_ref[...]
    table = wide_ref[...]
    owner, dep_row, dep_col = table[0:1], table[1:2], table[2:3]
    shift_row, shift_col, frac_row, frac_col = table[3:4], table[4:5], table[5:6], table[6:7]
    dep_tile = jnp.clip(band * tile_rows - 1 + dep_row, 0, last_row)
    start = TILE * (dep_tile - (group * PAIR * tile_rows - 1)) + shift_row - 1
    column = TILE * dep_col + shift_col - 1
    wrapped = jnp.where(dep_col == tile_cols - 1, TILE, 0)
    position = lax.rem(lax.broadcasted_iota(jnp.int32, (1, LANES), 1), tile_cols)
    turn = lax.bitwise_and(LANES + TILE * position - column, LANES - 1)
    shape = (INFO_ROWS, LANES)
    index = lax.broadcasted_iota(jnp.int32, shape, 0)
    lane = lax.broadcasted_iota(jnp.int32, shape, 1)
    info = jnp.zeros(shape, jnp.float32)
    for place, value in enumerate(cubic_weights(frac_row) + cubic_weights(frac_col)):
        info = jnp.where(index == place, value, info)
    places = jnp.zeros(shape, jnp.int32)
    for place, value in enumerate((start, owner, wrapped, turn)):
        places = jnp.where(index == place, value, places)
    info = jnp.where(lane < tiles, info, pltpu.roll(places.astype(jnp.float32), tiles, 1))
    for block in range(count):
        out_ref[block, TILE:, :] = info
    for copy in copies:
        copy.wait()


def parts(value):
    high = value.astype(jnp.bfloat16)
    return high, (value - high.astype(jnp.float32)).astype(jnp.bfloat16)


def tap_matrix():
    matrix = np.zeros((2 * LANES, (TAPS - 1) * LANES), np.float32)
    for tap in range(1, TAPS):
        for lane in range(LANES):
            odd = (lane // TILE) % 2
            matrix[odd * LANES + (lane + tap) % LANES, (tap - 1) * LANES + lane] = 1.0
    return jnp.asarray(matrix, jnp.bfloat16)


def beside_matrix():
    matrix = np.zeros((2 * LANES, LANES), np.float32)
    for lane in range(LANES):
        if lane > 0:
            matrix[lane - 1, lane] = 1.0
        if lane < LANES - 1:
            matrix[lane + 1, lane] = 1.0
    matrix[2 * LANES - 1, 0] = 1.0
    matrix[LANES, LANES - 1] = 1.0
    return jnp.asarray(np.concatenate([matrix, matrix]), jnp.bfloat16)


PAD = 8


def interpolate_kernel(
    places_ref, blocks_ref, rest_ref, north_ref, south_ref, taps_ref, phi_ref, top_ref, bottom_ref, ext_ref, pass_ref, sem
):
    chunks = north_ref.shape[0]
    rows = phi_ref.shape[1] - 2 * PAD
    cells = rows // PAIR
    tile_rows = cells // TILE
    tile_cols = LANES // TILE
    tiles = tile_rows * tile_cols
    north_half, south_half = slice(0, chunks), slice(chunks, 2 * chunks)
    sources = [
        north_ref,
        blocks_ref.at[north_half, 0:TILE, :],
        rest_ref.at[north_half],
        rest_ref.at[south_half],
        blocks_ref.at[south_half, 0:TILE, :],
        south_ref,
    ]
    copies = [
        pltpu.make_async_copy(source, ext_ref.at[:, place * TILE : (place + 1) * TILE, :], sem.at[place])
        for place, source in enumerate(sources)
    ]
    for copy in copies:
        copy.start()
    for chunk in range(chunks):
        phi_ref[chunk, 0:PAD, :] = jnp.zeros((PAD, LANES), jnp.float32)
        phi_ref[chunk, PAD + rows :, :] = jnp.zeros((PAD, LANES), jnp.float32)
    for copy in copies:
        copy.wait()
    lane = lax.broadcasted_iota(jnp.int32, (SPAN, LANES), 1)
    lane_info = lax.broadcasted_iota(jnp.int32, (INFO_ROWS, LANES), 1)
    first_even = lane < 48
    first_odd = (lane >= 16) & (lane < 80)
    even_group = lax.bitwise_and(lane, TILE) == 0
    together = pass_ref.shape[0] // tile_rows

    def windows(device, tile_row):
        def window(tile_col):
            tile = tile_row * tile_cols + tile_col
            start, source, wrapped, turn = (places_ref[device, place * tiles + tile] for place in range(4))
            after = lax.rem(source + 1, chunks)
            span = pl.ds(start, SPAN)
            return pltpu.roll(jnp.where(lane < wrapped, ext_ref[after, span, :], ext_ref[source, span, :]), turn, 1)

        return jnp.where(first_even, window(0), window(2)), jnp.where(first_odd, window(1), window(3))

    def step(index, carry):
        work = [(index * together + place, tile_row) for place in range(together) for tile_row in range(tile_rows)]
        pairs = [windows(*item) for item in work]
        evens = jnp.concatenate([pair[0] for pair in pairs], axis=0)
        odds = jnp.concatenate([pair[1] for pair in pairs], axis=0)
        even_parts, odd_parts = parts(evens), parts(odds)
        moved = None
        for which in range(2):
            part = jnp.dot(
                jnp.concatenate([even_parts[which], odd_parts[which]], axis=1),
                taps_ref[...],
                preferred_element_type=jnp.float32,
            )
            moved = part if moved is None else moved + part
        for slot, (device, tile_row) in enumerate(work):
            own = lane_info // TILE + tile_row * tile_cols
            weights = jnp.take_along_axis(blocks_ref[device, TILE:, :], own, axis=1)
            total = weights[TAPS : TAPS + 1] * jnp.where(even_group, *pairs[slot])
            here = slice(slot * SPAN, (slot + 1) * SPAN)
            for tap in range(1, TAPS):
                total = total + weights[TAPS + tap : TAPS + tap + 1] * moved[here, (tap - 1) * LANES : tap * LANES]
            pass_ref[slot] = total
            total = None
            for tap in range(TAPS):
                value = weights[tap : tap + 1] * pass_ref[slot, tap : tap + TILE, :]
                total = value if total is None else total + value
            first = pl.multiple_of(PAD + (device // chunks) * cells + tile_row * TILE, PAD)
            phi_ref[lax.rem(device, chunks), pl.ds(first, TILE), :] = total
        return carry

    lax.fori_loop(0, PAIR * chunks // together, step, 0)
    for row in range(2):
        for chunk in range(chunks):
            place = row * chunks + chunk
            top_ref[place : place + 1, :] = phi_ref[chunk, PAD + row : PAD + row + 1, :]
            bottom_ref[place : place + 1, :] = phi_ref[chunk, PAD + rows - 2 + row : PAD + rows - 1 + row, :]


def own_coef(coef_ref, half):
    levels = coef_ref.shape[1]
    member = lax.bitwise_xor(lax.axis_index("part"), swapped()) * half + lax.axis_index("lon")
    return coef_ref[member // levels, lax.rem(member, levels)]


TOGETHER = 8


def diffuse_kernel(groups, coef_ref, phi_ref, beside_ref, psi_ref, lap_ref, high_ref, low_ref):
    chunks, rows = phi_ref.shape[0], phi_ref.shape[1] - 2 * PAD
    cells = rows // PAIR
    coef = own_coef(coef_ref, chunks)
    group = lax.axis_index("group")
    has_north = jnp.where(group > 0, 1.0, 0.0)
    has_south = jnp.where(group < groups - 1, 1.0, 0.0)
    together = min(TOGETHER, chunks)

    def laplacian(ref, store):
        for chunk in range(chunks):
            high, low = parts(ref[chunk, PAD : PAD + rows, :])
            high_ref[chunk], low_ref[chunk] = high, low

        def step(index, carry):
            members = [index * together + place for place in range(together)]
            lane = lax.broadcasted_iota(jnp.int32, (rows, LANES), 1)
            left = []
            for part_ref in (high_ref, low_ref):
                left.append(jnp.concatenate([part_ref[chunk] for chunk in members], axis=0))
                left.append(
                    jnp.concatenate(
                        [
                            jnp.where(
                                lane == LANES - 1,
                                part_ref[lax.rem(chunk + chunks - 1, chunks)],
                                part_ref[lax.rem(chunk + 1, chunks)],
                            )
                            for chunk in members
                        ],
                        axis=0,
                    )
                )
            sums = jnp.dot(jnp.concatenate(left, axis=1), beside_ref[...], preferred_element_type=jnp.float32)
            for place, chunk in enumerate(members):
                around = ref[chunk, PAD + 1 : PAD + 1 + rows, :] + ref[chunk, PAD - 1 : PAD - 1 + rows, :]
                store(chunk, around + sums[place * rows : (place + 1) * rows] - 4.0 * ref[chunk, PAD : PAD + rows, :])
            return carry

        lax.fori_loop(0, chunks // together, step, 0)

    def keep(chunk, value):
        lap_ref[chunk, PAD : PAD + rows, :] = value
        lap_ref[chunk, PAD - 1 : PAD, :] = phi_ref[chunk, PAD : PAD + 1, :] * has_north
        lap_ref[chunk, PAD + rows : PAD + rows + 1, :] = phi_ref[chunk, PAD + rows - 1 : PAD + rows, :] * has_south

    def finish(chunk, value):
        psi = phi_ref[chunk, PAD : PAD + rows, :] - coef * value
        for band in range(PAIR):
            psi_ref[band * chunks + chunk] = psi[band * cells : (band + 1) * cells]

    laplacian(phi_ref, keep)
    laplacian(lap_ref, finish)


def mend_kernel(groups, coef_ref, north_ref, south_ref, inner_ref, psi_ref):
    count, cells = psi_ref.shape[0], psi_ref.shape[1]
    chunks = count // PAIR
    coef = own_coef(coef_ref, chunks)
    shape = (chunks, LANES)
    lane = lax.broadcasted_iota(jnp.int32, shape, 1)

    group = lax.axis_index("group")
    has_north = jnp.where(group > 0, 1.0, 0.0)
    has_south = jnp.where(group < groups - 1, 1.0, 0.0)

    def near_far(near, far, coef):
        west = pltpu.roll(jnp.where(lane == LANES - 1, pltpu.roll(near, 1, 0), near), 1, 1)
        east = pltpu.roll(jnp.where(lane == 0, pltpu.roll(near, chunks - 1, 0), near), LANES - 1, 1)
        return coef * (far + 2.0 * (west + east) - 8.0 * near), coef * near

    psi_ref[...] = inner_ref[...]
    north = near_far(north_ref[chunks:, :], north_ref[0:chunks, :], coef * has_north)
    south = near_far(south_ref[0:chunks, :], south_ref[chunks:, :], coef * has_south)
    for chunk in range(chunks):
        low = chunk + (PAIR - 1) * chunks
        for row in range(2):
            here = slice(row, row + 1)
            psi_ref[chunk, here, :] = inner_ref[chunk, here, :] - north[row][chunk : chunk + 1]
            here = slice(cells - 1 - row, cells - row)
            psi_ref[low, here, :] = inner_ref[low, here, :] - south[row][chunk : chunk + 1]


def vertical_kernel(lower_ref, upper_ref, inverse_ref, psi_ref, out_ref, held_ref, sem):
    fcount, levels, cells, _ = held_ref.shape
    step = 16
    copies = []
    swap = swapped()
    for field in range(fcount):
        source = lax.bitwise_xor(field, swap * (fcount // PAIR)) * levels
        for first in range(0, cells, step):
            rows = slice(first, first + step)
            sweep = []
            for level in range(levels):
                rhs = psi_ref[source + level, rows, :]
                if level:
                    rhs = rhs + lower_ref[field, level] * sweep[-1]
                sweep.append(rhs * inverse_ref[field, level])
            value = sweep[-1]
            held_ref[field, levels - 1, rows, :] = value
            for level in range(levels - 2, -1, -1):
                value = sweep[level] - upper_ref[field, level] * value
                held_ref[field, level, rows, :] = value
        copy = pltpu.make_async_copy(held_ref.at[field], out_ref.at[field], sem.at[field])
        copy.start()
        copies.append(copy)
    for copy in copies:
        copy.wait()


def vertical_tables(vert_coef):
    fcount = vert_coef.shape[0]
    levels = vert_coef.shape[1] + 1
    zero_column = jnp.zeros((fcount, 1), jnp.float32)
    lower_coef = jnp.concatenate([zero_column, vert_coef], axis=1)
    upper_coef = jnp.concatenate([vert_coef, zero_column], axis=1)
    diagonal = 1.0 + lower_coef + upper_coef
    uppers, inverses = [], []
    for level in range(levels):
        denominator = diagonal[:, level]
        if level:
            denominator = denominator + lower_coef[:, level] * uppers[-1]
        inverses.append(1.0 / denominator)
        uppers.append(-upper_coef[:, level] / denominator)
    return lower_coef, jnp.stack(uppers, axis=1), jnp.stack(inverses, axis=1)


SMEM = pltpu.MemorySpace.SMEM
VMEM = pltpu.MemorySpace.VMEM


def smem():
    return pl.BlockSpec(memory_space=SMEM)


def vmem():
    return pl.BlockSpec(memory_space=VMEM)


def anywhere():
    return pl.BlockSpec(memory_space=pl.ANY)


def body(fields, hyper_coef, vert_coef, dep_owner, dep_row, dep_col, shifts, fracs):
    fcount, levels, cells, width = fields.shape
    count = fcount * levels
    chunks = lax.axis_size("lon")
    groups = lax.axis_size("group")
    tile_rows = cells // TILE
    tile_cols = width // TILE
    tiles = tile_rows * tile_cols
    rows = PAIR * cells
    f32 = jnp.float32
    limit = pltpu.CompilerParams(vmem_limit_bytes=48 * 1024 * 1024)

    table = jnp.concatenate(
        [
            dep_owner.reshape(1, tiles),
            dep_row.reshape(1, tiles),
            dep_col.reshape(1, tiles),
            shifts.reshape(tiles, 2).T,
            fracs.reshape(tiles, 2).T,
        ],
        axis=0,
    )
    blocks, rest = pl.pallas_call(
        functools.partial(pack_kernel, tile_rows, tile_cols, groups * PAIR * tile_rows - 2),
        out_shape=(
            jax.ShapeDtypeStruct((count, TILE + INFO_ROWS, width), f32),
            jax.ShapeDtypeStruct((count, cells - TILE, width), f32),
        ),
        in_specs=[anywhere(), vmem()],
        out_specs=(vmem(), vmem()),
        scratch_shapes=[pltpu.VMEM((8, LANES), jnp.int32), pltpu.SemaphoreType.DMA((2 * PAIR,))],
        compiler_params=limit,
        name="pack",
    )(fields.reshape(count, cells, width), table)
    blocks = lax.all_to_all(blocks, ("part", "lon"), 0, 0, tiled=True)
    blocks, rest, vert_coef = lax.optimization_barrier((blocks, rest, vert_coef))
    rest = lax.all_to_all(rest, ("part", "lon"), 0, 0, tiled=True)
    southward = [
        (group * PAIR + part, (group + 1) % groups * PAIR + PAIR - 1 - part) for group in range(groups) for part in range(PAIR)
    ]
    northward = [(target, source) for source, target in southward]
    bands = ("group", "part")
    north = lax.ppermute(blocks[(PAIR - 1) * chunks :, :TILE, :], bands, southward)
    south = lax.ppermute(blocks[:chunks, :TILE, :], bands, northward)
    north, tables = lax.optimization_barrier((north, vertical_tables(vert_coef)))
    places = blocks[:, TILE : TILE + 4, tiles : 2 * tiles].astype(jnp.int32).reshape(PAIR * chunks, 4 * tiles)
    edge = jax.ShapeDtypeStruct((2 * chunks, width), f32)
    phi, top, bottom = pl.pallas_call(
        interpolate_kernel,
        out_shape=(jax.ShapeDtypeStruct((chunks, rows + 2 * PAD, width), f32), edge, edge),
        in_specs=[smem(), vmem(), vmem(), vmem(), vmem(), vmem()],
        out_specs=(vmem(), vmem(), vmem()),
        scratch_shapes=[
            pltpu.VMEM((chunks, rows + 2 * TILE + 8, width), f32),
            pltpu.VMEM((min(16, chunks) * tile_rows, SPAN, width), f32),
            pltpu.SemaphoreType.DMA((2 + 2 * PAIR,)),
        ],
        compiler_params=limit,
        name="interpolate",
    )(places, blocks, rest, north, south, tap_matrix())
    above = lax.ppermute(bottom, bands, southward)
    below = lax.ppermute(top, bands, northward)
    psi_shape = jax.ShapeDtypeStruct((count, cells, width), f32)
    inner = pl.pallas_call(
        functools.partial(diffuse_kernel, groups),
        out_shape=psi_shape,
        in_specs=[smem(), vmem(), vmem()],
        out_specs=vmem(),
        scratch_shapes=[
            pltpu.VMEM((chunks, rows + 2 * PAD, width), f32),
            pltpu.VMEM((chunks, rows, width), jnp.bfloat16),
            pltpu.VMEM((chunks, rows, width), jnp.bfloat16),
        ],
        compiler_params=limit,
        name="diffuse",
    )(hyper_coef, phi, beside_matrix())
    psi = pl.pallas_call(
        functools.partial(mend_kernel, groups),
        out_shape=psi_shape,
        in_specs=[smem(), vmem(), vmem(), vmem()],
        out_specs=vmem(),
        compiler_params=limit,
        name="mend",
    )(hyper_coef, above, below, inner)
    psi = lax.all_to_all(psi, ("part", "lon"), 0, 0, tiled=True)
    return pl.pallas_call(
        vertical_kernel,
        out_shape=jax.ShapeDtypeStruct((fcount, levels, cells, width), f32),
        in_specs=[smem(), smem(), smem(), vmem()],
        out_specs=anywhere(),
        scratch_shapes=[pltpu.VMEM((fcount, levels, cells, width), f32), pltpu.SemaphoreType.DMA((fcount,))],
        compiler_params=limit,
        name="solve",
    )(*tables, psi)


def solution(mesh):
    lat, lon = mesh.shape["lat"], mesh.shape["lon"]
    grouped = Mesh(mesh.devices.reshape(lat // PAIR, PAIR, lon), ("group", "part", "lon"))
    bands = ("group", "part")
    cells = P(None, None, bands, "lon")
    tiles = P(bands, "lon", None, None)
    return jax.shard_map(
        body,
        mesh=grouped,
        in_specs=(cells, P(), P(), tiles, tiles, tiles, tiles, tiles),
        out_specs=cells,
        check_vma=False,
    )
```

```python
import functools

import jax
import jax.numpy as jnp
import numpy as np
from jax import lax
from jax.experimental import pallas as pl
from jax.experimental.pallas import tpu as pltpu
from jax.sharding import Mesh, PartitionSpec as P

TILE = 32
FRACS = 16
LANES = 128
INFO_ROWS = 8
PAIR = 2
TAPS = 4
SPAN = 40


def cubic_weights(fraction_index):
    fraction = fraction_index.astype(jnp.float32) / FRACS
    return (
        -fraction * (fraction - 1.0) * (fraction - 2.0) / 6.0,
        (fraction + 1.0) * (fraction - 1.0) * (fraction - 2.0) / 2.0,
        -(fraction + 1.0) * fraction * (fraction - 2.0) / 2.0,
        (fraction + 1.0) * fraction * (fraction - 1.0) / 6.0,
    )


def swapped():
    return lax.rem(lax.axis_index("group"), 2)


def pack_kernel(tile_rows, tile_cols, last_row, fields_ref, table_ref, out_ref, rest_ref, wide_ref, sem):
    count = fields_ref.shape[0]
    half = count // PAIR
    swap = swapped()
    group = lax.axis_index("group")
    part = lax.axis_index("part")
    border = pl.ds(pl.multiple_of(part * TILE, TILE), TILE)
    inner = pl.ds(pl.multiple_of((1 - part) * TILE, TILE), TILE)
    copies = []
    for place in range(PAIR):
        source = pl.ds(lax.bitwise_xor(place, swap) * half, half)
        blocks = slice(place * half, (place + 1) * half)
        copies.append(pltpu.make_async_copy(fields_ref.at[source, border], out_ref.at[blocks], sem.at[2 * place]))
        copies.append(pltpu.make_async_copy(fields_ref.at[source, inner], rest_ref.at[blocks, 0:TILE, :], sem.at[2 * place + 1]))
    for copy in copies:
        copy.start()
    entries, tiles = table_ref.shape
    band = group * PAIR + part
    wide_ref[...] = jnp.zeros(wide_ref.shape, jnp.int32)
    wide_ref[0:entries, 0:tiles] = table_ref[...]
    table = wide_ref[...]
    owner, dep_row, dep_col = table[0:1], table[1:2], table[2:3]
    shift_row, shift_col, frac_row, frac_col = table[3:4], table[4:5], table[5:6], table[6:7]
    dep_tile = jnp.clip(band * tile_rows - 1 + dep_row, 0, last_row)
    start = TILE * (dep_tile - (group * PAIR * tile_rows - 1)) + shift_row - 1
    column = TILE * dep_col + shift_col - 1
    wrapped = jnp.where(dep_col == tile_cols - 1, TILE, 0)
    position = lax.rem(lax.broadcasted_iota(jnp.int32, (1, LANES), 1), tile_cols)
    turn = lax.bitwise_and(LANES + TILE * position - column, LANES - 1)
    shape = (INFO_ROWS, LANES)
    index = lax.broadcasted_iota(jnp.int32, shape, 0)
    lane = lax.broadcasted_iota(jnp.int32, shape, 1)
    info = jnp.zeros(shape, jnp.float32)
    for place, value in enumerate(cubic_weights(frac_row) + cubic_weights(frac_col)):
        info = jnp.where(index == place, value, info)
    for place, value in enumerate((start, owner, wrapped, turn)):
        first = tiles * (place + 1)
        value = pltpu.roll(value.astype(jnp.float32), first, 1)
        info = jnp.where((index == 0) & (lane >= first) & (lane < first + tiles), value, info)
    for block in range(count):
        rest_ref[block, TILE:, :] = info
    for copy in copies:
        copy.wait()


def parts(value):
    high = value.astype(jnp.bfloat16)
    return high, (value - high.astype(jnp.float32)).astype(jnp.bfloat16)


def tap_matrix():
    matrix = np.zeros((2 * LANES, (TAPS - 1) * LANES), np.float32)
    for tap in range(1, TAPS):
        for lane in range(LANES):
            odd = (lane // TILE) % 2
            matrix[odd * LANES + (lane + tap) % LANES, (tap - 1) * LANES + lane] = 1.0
    return jnp.asarray(matrix, jnp.bfloat16)


def beside_matrix():
    matrix = np.zeros((2 * LANES, LANES), np.float32)
    for lane in range(LANES):
        if lane > 0:
            matrix[lane - 1, lane] = 1.0
        if lane < LANES - 1:
            matrix[lane + 1, lane] = 1.0
    matrix[2 * LANES - 1, 0] = 1.0
    matrix[LANES, LANES - 1] = 1.0
    return jnp.asarray(np.concatenate([matrix, matrix]), jnp.bfloat16)


PAD = 8


def interpolate_kernel(
    places_ref, blocks_ref, rest_ref, north_ref, south_ref, taps_ref, phi_ref, top_ref, bottom_ref, ext_ref, pass_ref, sem
):
    chunks = north_ref.shape[0]
    rows = phi_ref.shape[1] - 2 * PAD
    cells = rows // PAIR
    tile_rows = cells // TILE
    tile_cols = LANES // TILE
    tiles = tile_rows * tile_cols
    north_half, south_half = slice(0, chunks), slice(chunks, 2 * chunks)
    sources = [
        north_ref,
        blocks_ref.at[north_half],
        rest_ref.at[north_half, 0:TILE, :],
        rest_ref.at[south_half, 0:TILE, :],
        blocks_ref.at[south_half],
        south_ref,
    ]
    copies = [
        pltpu.make_async_copy(source, ext_ref.at[:, place * TILE : (place + 1) * TILE, :], sem.at[place])
        for place, source in enumerate(sources)
    ]
    for copy in copies:
        copy.start()
    for chunk in range(chunks):
        phi_ref[chunk, 0:PAD, :] = jnp.zeros((PAD, LANES), jnp.float32)
        phi_ref[chunk, PAD + rows :, :] = jnp.zeros((PAD, LANES), jnp.float32)
    for copy in copies:
        copy.wait()
    lane = lax.broadcasted_iota(jnp.int32, (SPAN, LANES), 1)
    lane_info = lax.broadcasted_iota(jnp.int32, (INFO_ROWS, LANES), 1)
    first_even = lane < 48
    first_odd = (lane >= 16) & (lane < 80)
    even_group = lax.bitwise_and(lane, TILE) == 0
    together = pass_ref.shape[0] // tile_rows

    def windows(device, tile_row):
        def window(tile_col):
            tile = tile_row * tile_cols + tile_col
            start, source, wrapped, turn = (places_ref[device, tiles * place + tile] for place in range(4))
            after = lax.rem(source + 1, chunks)
            span = pl.ds(start, SPAN)
            return pltpu.roll(jnp.where(lane < wrapped, ext_ref[after, span, :], ext_ref[source, span, :]), turn, 1)

        return jnp.where(first_even, window(0), window(2)), jnp.where(first_odd, window(1), window(3))

    def step(index, carry):
        work = [(index * together + place, tile_row) for place in range(together) for tile_row in range(tile_rows)]
        pairs = [windows(*item) for item in work]
        evens = jnp.concatenate([pair[0] for pair in pairs], axis=0)
        odds = jnp.concatenate([pair[1] for pair in pairs], axis=0)
        even_parts, odd_parts = parts(evens), parts(odds)
        moved = None
        for which in range(2):
            part = jnp.dot(
                jnp.concatenate([even_parts[which], odd_parts[which]], axis=1),
                taps_ref[...],
                preferred_element_type=jnp.float32,
            )
            moved = part if moved is None else moved + part
        for slot, (device, tile_row) in enumerate(work):
            own = lane_info // TILE + tile_row * tile_cols
            weights = jnp.take_along_axis(rest_ref[device, TILE:, :], own, axis=1)
            total = weights[TAPS : TAPS + 1] * jnp.where(even_group, *pairs[slot])
            here = slice(slot * SPAN, (slot + 1) * SPAN)
            for tap in range(1, TAPS):
                total = total + weights[TAPS + tap : TAPS + tap + 1] * moved[here, (tap - 1) * LANES : tap * LANES]
            pass_ref[slot] = total
            total = None
            for tap in range(TAPS):
                value = weights[tap : tap + 1] * pass_ref[slot, tap : tap + TILE, :]
                total = value if total is None else total + value
            first = pl.multiple_of(PAD + (device // chunks) * cells + tile_row * TILE, PAD)
            phi_ref[lax.rem(device, chunks), pl.ds(first, TILE), :] = total
        return carry

    lax.fori_loop(0, PAIR * chunks // together, step, 0)
    for row in range(2):
        for chunk in range(chunks):
            place = row * chunks + chunk
            top_ref[place : place + 1, :] = phi_ref[chunk, PAD + row : PAD + row + 1, :]
            bottom_ref[place : place + 1, :] = phi_ref[chunk, PAD + rows - 2 + row : PAD + rows - 1 + row, :]


def own_coef(coef_ref, half):
    levels = coef_ref.shape[1]
    member = lax.bitwise_xor(lax.axis_index("part"), swapped()) * half + lax.axis_index("lon")
    return coef_ref[member // levels, lax.rem(member, levels)]


TOGETHER = 16


def diffuse_kernel(groups, coef_ref, phi_ref, beside_ref, psi_ref, lap_ref, high_ref, low_ref):
    chunks, rows = phi_ref.shape[0], phi_ref.shape[1] - 2 * PAD
    cells = rows // PAIR
    coef = own_coef(coef_ref, chunks)
    group = lax.axis_index("group")
    has_north = jnp.where(group > 0, 1.0, 0.0)
    has_south = jnp.where(group < groups - 1, 1.0, 0.0)
    together = min(TOGETHER, chunks)

    def laplacian(ref, store):
        for chunk in range(chunks):
            high, low = parts(ref[chunk, PAD : PAD + rows, :])
            high_ref[chunk], low_ref[chunk] = high, low

        def step(index, carry):
            members = [index * together + place for place in range(together)]
            lane = lax.broadcasted_iota(jnp.int32, (rows, LANES), 1)
            left = []
            for part_ref in (high_ref, low_ref):
                left.append(jnp.concatenate([part_ref[chunk] for chunk in members], axis=0))
                left.append(
                    jnp.concatenate(
                        [
                            jnp.where(
                                lane == LANES - 1,
                                part_ref[lax.rem(chunk + chunks - 1, chunks)],
                                part_ref[lax.rem(chunk + 1, chunks)],
                            )
                            for chunk in members
                        ],
                        axis=0,
                    )
                )
            sums = jnp.dot(jnp.concatenate(left, axis=1), beside_ref[...], preferred_element_type=jnp.float32)
            for place, chunk in enumerate(members):
                around = ref[chunk, PAD + 1 : PAD + 1 + rows, :] + ref[chunk, PAD - 1 : PAD - 1 + rows, :]
                store(chunk, around + sums[place * rows : (place + 1) * rows] - 4.0 * ref[chunk, PAD : PAD + rows, :])
            return carry

        lax.fori_loop(0, chunks // together, step, 0)

    def keep(chunk, value):
        lap_ref[chunk, PAD : PAD + rows, :] = value
        lap_ref[chunk, PAD - 1 : PAD, :] = phi_ref[chunk, PAD : PAD + 1, :] * has_north
        lap_ref[chunk, PAD + rows : PAD + rows + 1, :] = phi_ref[chunk, PAD + rows - 1 : PAD + rows, :] * has_south

    def finish(chunk, value):
        psi = phi_ref[chunk, PAD : PAD + rows, :] - coef * value
        for band in range(PAIR):
            psi_ref[band * chunks + chunk] = psi[band * cells : (band + 1) * cells]

    laplacian(phi_ref, keep)
    laplacian(lap_ref, finish)


def mend_kernel(groups, coef_ref, north_ref, south_ref, inner_ref, psi_ref):
    count, cells = psi_ref.shape[0], psi_ref.shape[1]
    chunks = count // PAIR
    coef = own_coef(coef_ref, chunks)
    shape = (chunks, LANES)
    lane = lax.broadcasted_iota(jnp.int32, shape, 1)

    group = lax.axis_index("group")
    has_north = jnp.where(group > 0, 1.0, 0.0)
    has_south = jnp.where(group < groups - 1, 1.0, 0.0)

    def near_far(near, far, coef):
        west = pltpu.roll(jnp.where(lane == LANES - 1, pltpu.roll(near, 1, 0), near), 1, 1)
        east = pltpu.roll(jnp.where(lane == 0, pltpu.roll(near, chunks - 1, 0), near), LANES - 1, 1)
        return coef * (far + 2.0 * (west + east) - 8.0 * near), coef * near

    psi_ref[...] = inner_ref[...]
    north = near_far(north_ref[chunks:, :], north_ref[0:chunks, :], coef * has_north)
    south = near_far(south_ref[0:chunks, :], south_ref[chunks:, :], coef * has_south)
    for chunk in range(chunks):
        low = chunk + (PAIR - 1) * chunks
        for row in range(2):
            here = slice(row, row + 1)
            psi_ref[chunk, here, :] = inner_ref[chunk, here, :] - north[row][chunk : chunk + 1]
            here = slice(cells - 1 - row, cells - row)
            psi_ref[low, here, :] = inner_ref[low, here, :] - south[row][chunk : chunk + 1]


def vertical_kernel(lower_ref, upper_ref, inverse_ref, psi_ref, out_ref, held_ref, sem):
    fcount, levels, cells, _ = held_ref.shape
    step = 16
    copies = []
    swap = swapped()
    for field in range(fcount):
        source = lax.bitwise_xor(field, swap * (fcount // PAIR)) * levels
        for first in range(0, cells, step):
            rows = slice(first, first + step)
            sweep = []
            for level in range(levels):
                rhs = psi_ref[source + level, rows, :]
                if level:
                    rhs = rhs + lower_ref[field, level] * sweep[-1]
                sweep.append(rhs * inverse_ref[field, level])
            value = sweep[-1]
            held_ref[field, levels - 1, rows, :] = value
            for level in range(levels - 2, -1, -1):
                value = sweep[level] - upper_ref[field, level] * value
                held_ref[field, level, rows, :] = value
        copy = pltpu.make_async_copy(held_ref.at[field], out_ref.at[field], sem.at[field])
        copy.start()
        copies.append(copy)
    for copy in copies:
        copy.wait()


def vertical_tables(vert_coef):
    fcount = vert_coef.shape[0]
    levels = vert_coef.shape[1] + 1
    zero_column = jnp.zeros((fcount, 1), jnp.float32)
    lower_coef = jnp.concatenate([zero_column, vert_coef], axis=1)
    upper_coef = jnp.concatenate([vert_coef, zero_column], axis=1)
    diagonal = 1.0 + lower_coef + upper_coef
    uppers, inverses = [], []
    for level in range(levels):
        denominator = diagonal[:, level]
        if level:
            denominator = denominator + lower_coef[:, level] * uppers[-1]
        inverses.append(1.0 / denominator)
        uppers.append(-upper_coef[:, level] / denominator)
    return lower_coef, jnp.stack(uppers, axis=1), jnp.stack(inverses, axis=1)


SMEM = pltpu.MemorySpace.SMEM
VMEM = pltpu.MemorySpace.VMEM


def smem():
    return pl.BlockSpec(memory_space=SMEM)


def vmem():
    return pl.BlockSpec(memory_space=VMEM)


def anywhere():
    return pl.BlockSpec(memory_space=pl.ANY)


def body(fields, hyper_coef, vert_coef, dep_owner, dep_row, dep_col, shifts, fracs):
    fcount, levels, cells, width = fields.shape
    count = fcount * levels
    chunks = lax.axis_size("lon")
    groups = lax.axis_size("group")
    tile_rows = cells // TILE
    tile_cols = width // TILE
    tiles = tile_rows * tile_cols
    rows = PAIR * cells
    f32 = jnp.float32
    limit = pltpu.CompilerParams(vmem_limit_bytes=48 * 1024 * 1024)

    table = jnp.concatenate(
        [
            dep_owner.reshape(1, tiles),
            dep_row.reshape(1, tiles),
            dep_col.reshape(1, tiles),
            shifts.reshape(tiles, 2).T,
            fracs.reshape(tiles, 2).T,
        ],
        axis=0,
    )
    blocks, rest = pl.pallas_call(
        functools.partial(pack_kernel, tile_rows, tile_cols, groups * PAIR * tile_rows - 2),
        out_shape=(
            jax.ShapeDtypeStruct((count, TILE, width), f32),
            jax.ShapeDtypeStruct((count, cells - TILE + INFO_ROWS, width), f32),
        ),
        in_specs=[anywhere(), vmem()],
        out_specs=(vmem(), vmem()),
        scratch_shapes=[pltpu.VMEM((8, LANES), jnp.int32), pltpu.SemaphoreType.DMA((2 * PAIR,))],
        compiler_params=limit,
        name="pack",
    )(fields.reshape(count, cells, width), table)
    blocks = lax.all_to_all(blocks, ("part", "lon"), 0, 0, tiled=True)
    blocks, rest, vert_coef = lax.optimization_barrier((blocks, rest, vert_coef))
    rest = lax.all_to_all(rest, ("part", "lon"), 0, 0, tiled=True)
    tables = vertical_tables(vert_coef)
    ready, tables = lax.optimization_barrier((blocks, tables))
    southward = [
        (group * PAIR + part, (group + 1) % groups * PAIR + PAIR - 1 - part) for group in range(groups) for part in range(PAIR)
    ]
    northward = [(target, source) for source, target in southward]
    bands = ("group", "part")
    north = lax.ppermute(ready[(PAIR - 1) * chunks :, :TILE, :], bands, southward)
    south = lax.ppermute(ready[:chunks, :TILE, :], bands, northward)
    places = rest[:, cells - TILE, tiles : 5 * tiles].astype(jnp.int32)
    edge = jax.ShapeDtypeStruct((2 * chunks, width), f32)
    phi, top, bottom = pl.pallas_call(
        interpolate_kernel,
        out_shape=(jax.ShapeDtypeStruct((chunks, rows + 2 * PAD, width), f32), edge, edge),
        in_specs=[smem()] + [vmem()] * 5,
        out_specs=(vmem(), vmem(), vmem()),
        scratch_shapes=[
            pltpu.VMEM((chunks, rows + 2 * TILE + 8, width), f32),
            pltpu.VMEM((min(16, chunks) * tile_rows, SPAN, width), f32),
            pltpu.SemaphoreType.DMA((2 + 2 * PAIR,)),
        ],
        compiler_params=limit,
        name="interpolate",
    )(places, blocks, rest, north, south, tap_matrix())
    above = lax.ppermute(bottom, bands, southward)
    below = lax.ppermute(top, bands, northward)
    psi_shape = jax.ShapeDtypeStruct((count, cells, width), f32)
    inner = pl.pallas_call(
        functools.partial(diffuse_kernel, groups),
        out_shape=psi_shape,
        in_specs=[smem(), vmem(), vmem()],
        out_specs=vmem(),
        scratch_shapes=[
            pltpu.VMEM((chunks, rows + 2 * PAD, width), f32),
            pltpu.VMEM((chunks, rows, width), jnp.bfloat16),
            pltpu.VMEM((chunks, rows, width), jnp.bfloat16),
        ],
        compiler_params=limit,
        name="diffuse",
    )(hyper_coef, phi, beside_matrix())
    psi = pl.pallas_call(
        functools.partial(mend_kernel, groups),
        out_shape=psi_shape,
        in_specs=[smem(), vmem(), vmem(), vmem()],
        out_specs=vmem(),
        compiler_params=limit,
        name="mend",
    )(hyper_coef, above, below, inner)
    psi = lax.all_to_all(psi, ("part", "lon"), 0, 0, tiled=True)
    return pl.pallas_call(
        vertical_kernel,
        out_shape=jax.ShapeDtypeStruct((fcount, levels, cells, width), f32),
        in_specs=[smem(), smem(), smem(), vmem()],
        out_specs=anywhere(),
        scratch_shapes=[pltpu.VMEM((fcount, levels, cells, width), f32), pltpu.SemaphoreType.DMA((fcount,))],
        compiler_params=limit,
        name="solve",
    )(*tables, psi)


def solution(mesh):
    lat, lon = mesh.shape["lat"], mesh.shape["lon"]
    grouped = Mesh(mesh.devices.reshape(lat // PAIR, PAIR, lon), ("group", "part", "lon"))
    bands = ("group", "part")
    cells = P(None, None, bands, "lon")
    tiles = P(bands, "lon", None, None)
    return jax.shard_map(
        body,
        mesh=grouped,
        in_specs=(cells, P(), P(), tiles, tiles, tiles, tiles, tiles),
        out_specs=cells,
        check_vma=False,
    )
```

```python
import functools

import jax
import jax.numpy as jnp
import numpy as np
from jax import lax
from jax.experimental import pallas as pl
from jax.experimental.pallas import tpu as pltpu
from jax.sharding import Mesh, PartitionSpec as P

TILE = 32
FRACS = 16
LANES = 128
INFO_ROWS = 8
PAIR = 2
TAPS = 4
SPAN = 40


def cubic_weights(fraction_index):
    fraction = fraction_index.astype(jnp.float32) / FRACS
    return (
        -fraction * (fraction - 1.0) * (fraction - 2.0) / 6.0,
        (fraction + 1.0) * (fraction - 1.0) * (fraction - 2.0) / 2.0,
        -(fraction + 1.0) * fraction * (fraction - 2.0) / 2.0,
        (fraction + 1.0) * fraction * (fraction - 1.0) / 6.0,
    )


def swapped():
    return lax.rem(lax.axis_index("group"), 2)


def block_copies(fields_ref, place, out_ref, sem):
    half = fields_ref.shape[0] // PAIR
    rows = pl.ds(pl.multiple_of(place * TILE, TILE), TILE)
    return [
        pltpu.make_async_copy(
            fields_ref.at[pl.ds(lax.bitwise_xor(part, swapped()) * half, half), rows],
            out_ref.at[part * half : (part + 1) * half, 0:TILE, :],
            sem.at[part],
        )
        for part in range(PAIR)
    ]


def pack_border_kernel(fields_ref, out_ref, sem):
    copies = block_copies(fields_ref, lax.axis_index("part"), out_ref, sem)
    for copy in copies:
        copy.start()
    for copy in copies:
        copy.wait()


def pack_inner_kernel(tile_rows, tile_cols, last_row, fields_ref, table_ref, rest_ref, wide_ref, sem):
    count = fields_ref.shape[0]
    group = lax.axis_index("group")
    part = lax.axis_index("part")
    copies = block_copies(fields_ref, 1 - part, rest_ref, sem)
    for copy in copies:
        copy.start()
    entries, tiles = table_ref.shape
    band = group * PAIR + part
    wide_ref[...] = jnp.zeros(wide_ref.shape, jnp.int32)
    wide_ref[0:entries, 0:tiles] = table_ref[...]
    table = wide_ref[...]
    owner, dep_row, dep_col = table[0:1], table[1:2], table[2:3]
    shift_row, shift_col, frac_row, frac_col = table[3:4], table[4:5], table[5:6], table[6:7]
    dep_tile = jnp.clip(band * tile_rows - 1 + dep_row, 0, last_row)
    start = TILE * (dep_tile - (group * PAIR * tile_rows - 1)) + shift_row - 1
    column = TILE * dep_col + shift_col - 1
    wrapped = jnp.where(dep_col == tile_cols - 1, TILE, 0)
    position = lax.rem(lax.broadcasted_iota(jnp.int32, (1, LANES), 1), tile_cols)
    turn = lax.bitwise_and(LANES + TILE * position - column, LANES - 1)
    shape = (INFO_ROWS, LANES)
    index = lax.broadcasted_iota(jnp.int32, shape, 0)
    lane = lax.broadcasted_iota(jnp.int32, shape, 1)
    info = jnp.zeros(shape, jnp.float32)
    for place, value in enumerate(cubic_weights(frac_row) + cubic_weights(frac_col)):
        info = jnp.where(index == place, value, info)
    for place, value in enumerate((start, owner, wrapped, turn)):
        first = tiles * (place + 1)
        value = pltpu.roll(value.astype(jnp.float32), first, 1)
        info = jnp.where((index == 0) & (lane >= first) & (lane < first + tiles), value, info)
    for block in range(count):
        rest_ref[block, TILE:, :] = info
    for copy in copies:
        copy.wait()


def parts(value):
    high = value.astype(jnp.bfloat16)
    return high, (value - high.astype(jnp.float32)).astype(jnp.bfloat16)


def tap_matrix():
    matrix = np.zeros((2 * LANES, (TAPS - 1) * LANES), np.float32)
    for tap in range(1, TAPS):
        for lane in range(LANES):
            odd = (lane // TILE) % 2
            matrix[odd * LANES + (lane + tap) % LANES, (tap - 1) * LANES + lane] = 1.0
    return jnp.asarray(matrix, jnp.bfloat16)


def beside_matrix():
    matrix = np.zeros((2 * LANES, LANES), np.float32)
    for lane in range(LANES):
        if lane > 0:
            matrix[lane - 1, lane] = 1.0
        if lane < LANES - 1:
            matrix[lane + 1, lane] = 1.0
    matrix[2 * LANES - 1, 0] = 1.0
    matrix[LANES, LANES - 1] = 1.0
    return jnp.asarray(np.concatenate([matrix, matrix]), jnp.bfloat16)


PAD = 8


def interpolate_kernel(
    places_ref, blocks_ref, rest_ref, north_ref, south_ref, taps_ref, phi_ref, top_ref, bottom_ref, ext_ref, pass_ref, sem
):
    chunks = north_ref.shape[0]
    rows = phi_ref.shape[1] - 2 * PAD
    cells = rows // PAIR
    tile_rows = cells // TILE
    tile_cols = LANES // TILE
    tiles = tile_rows * tile_cols
    north_half, south_half = slice(0, chunks), slice(chunks, 2 * chunks)
    sources = [
        north_ref,
        blocks_ref.at[north_half],
        rest_ref.at[north_half, 0:TILE, :],
        rest_ref.at[south_half, 0:TILE, :],
        blocks_ref.at[south_half],
        south_ref,
    ]
    copies = [
        pltpu.make_async_copy(source, ext_ref.at[:, place * TILE : (place + 1) * TILE, :], sem.at[place])
        for place, source in enumerate(sources)
    ]
    for copy in copies:
        copy.start()
    for chunk in range(chunks):
        phi_ref[chunk, 0:PAD, :] = jnp.zeros((PAD, LANES), jnp.float32)
        phi_ref[chunk, PAD + rows :, :] = jnp.zeros((PAD, LANES), jnp.float32)
    for copy in copies:
        copy.wait()
    lane = lax.broadcasted_iota(jnp.int32, (SPAN, LANES), 1)
    lane_info = lax.broadcasted_iota(jnp.int32, (INFO_ROWS, LANES), 1)
    first_even = lane < 48
    first_odd = (lane >= 16) & (lane < 80)
    even_group = lax.bitwise_and(lane, TILE) == 0
    together = pass_ref.shape[0] // tile_rows

    def windows(device, tile_row):
        def window(tile_col):
            tile = tile_row * tile_cols + tile_col
            start, source, wrapped, turn = (places_ref[device, tiles * place + tile] for place in range(4))
            after = lax.rem(source + 1, chunks)
            span = pl.ds(start, SPAN)
            return pltpu.roll(jnp.where(lane < wrapped, ext_ref[after, span, :], ext_ref[source, span, :]), turn, 1)

        return jnp.where(first_even, window(0), window(2)), jnp.where(first_odd, window(1), window(3))

    def step(index, carry):
        work = [(index * together + place, tile_row) for place in range(together) for tile_row in range(tile_rows)]
        pairs = [windows(*item) for item in work]
        evens = jnp.concatenate([pair[0] for pair in pairs], axis=0)
        odds = jnp.concatenate([pair[1] for pair in pairs], axis=0)
        even_parts, odd_parts = parts(evens), parts(odds)
        moved = None
        for which in range(2):
            part = jnp.dot(
                jnp.concatenate([even_parts[which], odd_parts[which]], axis=1),
                taps_ref[...],
                preferred_element_type=jnp.float32,
            )
            moved = part if moved is None else moved + part
        for slot, (device, tile_row) in enumerate(work):
            own = lane_info // TILE + tile_row * tile_cols
            weights = jnp.take_along_axis(rest_ref[device, TILE:, :], own, axis=1)
            total = weights[TAPS : TAPS + 1] * jnp.where(even_group, *pairs[slot])
            here = slice(slot * SPAN, (slot + 1) * SPAN)
            for tap in range(1, TAPS):
                total = total + weights[TAPS + tap : TAPS + tap + 1] * moved[here, (tap - 1) * LANES : tap * LANES]
            pass_ref[slot] = total
            total = None
            for tap in range(TAPS):
                value = weights[tap : tap + 1] * pass_ref[slot, tap : tap + TILE, :]
                total = value if total is None else total + value
            first = pl.multiple_of(PAD + (device // chunks) * cells + tile_row * TILE, PAD)
            phi_ref[lax.rem(device, chunks), pl.ds(first, TILE), :] = total
        return carry

    lax.fori_loop(0, PAIR * chunks // together, step, 0)
    for row in range(2):
        for chunk in range(chunks):
            place = row * chunks + chunk
            top_ref[place : place + 1, :] = phi_ref[chunk, PAD + row : PAD + row + 1, :]
            bottom_ref[place : place + 1, :] = phi_ref[chunk, PAD + rows - 2 + row : PAD + rows - 1 + row, :]


def own_coef(coef_ref, half):
    levels = coef_ref.shape[1]
    member = lax.bitwise_xor(lax.axis_index("part"), swapped()) * half + lax.axis_index("lon")
    return coef_ref[member // levels, lax.rem(member, levels)]


TOGETHER = 16


def diffuse_kernel(groups, coef_ref, phi_ref, beside_ref, psi_ref, lap_ref, high_ref, low_ref):
    chunks, rows = phi_ref.shape[0], phi_ref.shape[1] - 2 * PAD
    cells = rows // PAIR
    coef = own_coef(coef_ref, chunks)
    group = lax.axis_index("group")
    has_north = jnp.where(group > 0, 1.0, 0.0)
    has_south = jnp.where(group < groups - 1, 1.0, 0.0)
    together = min(TOGETHER, chunks)

    def laplacian(ref, store):
        for chunk in range(chunks):
            high, low = parts(ref[chunk, PAD : PAD + rows, :])
            high_ref[chunk], low_ref[chunk] = high, low

        def step(index, carry):
            members = [index * together + place for place in range(together)]
            lane = lax.broadcasted_iota(jnp.int32, (rows, LANES), 1)
            left = []
            for part_ref in (high_ref, low_ref):
                left.append(jnp.concatenate([part_ref[chunk] for chunk in members], axis=0))
                left.append(
                    jnp.concatenate(
                        [
                            jnp.where(
                                lane == LANES - 1,
                                part_ref[lax.rem(chunk + chunks - 1, chunks)],
                                part_ref[lax.rem(chunk + 1, chunks)],
                            )
                            for chunk in members
                        ],
                        axis=0,
                    )
                )
            sums = jnp.dot(jnp.concatenate(left, axis=1), beside_ref[...], preferred_element_type=jnp.float32)
            for place, chunk in enumerate(members):
                around = ref[chunk, PAD + 1 : PAD + 1 + rows, :] + ref[chunk, PAD - 1 : PAD - 1 + rows, :]
                store(chunk, around + sums[place * rows : (place + 1) * rows] - 4.0 * ref[chunk, PAD : PAD + rows, :])
            return carry

        lax.fori_loop(0, chunks // together, step, 0)

    def keep(chunk, value):
        lap_ref[chunk, PAD : PAD + rows, :] = value
        lap_ref[chunk, PAD - 1 : PAD, :] = phi_ref[chunk, PAD : PAD + 1, :] * has_north
        lap_ref[chunk, PAD + rows : PAD + rows + 1, :] = phi_ref[chunk, PAD + rows - 1 : PAD + rows, :] * has_south

    def finish(chunk, value):
        psi = phi_ref[chunk, PAD : PAD + rows, :] - coef * value
        for band in range(PAIR):
            psi_ref[band * chunks + chunk] = psi[band * cells : (band + 1) * cells]

    laplacian(phi_ref, keep)
    laplacian(lap_ref, finish)


def mend_kernel(groups, coef_ref, north_ref, south_ref, inner_ref, psi_ref):
    count, cells = psi_ref.shape[0], psi_ref.shape[1]
    chunks = count // PAIR
    coef = own_coef(coef_ref, chunks)
    shape = (chunks, LANES)
    lane = lax.broadcasted_iota(jnp.int32, shape, 1)

    group = lax.axis_index("group")
    has_north = jnp.where(group > 0, 1.0, 0.0)
    has_south = jnp.where(group < groups - 1, 1.0, 0.0)

    def near_far(near, far, coef):
        west = pltpu.roll(jnp.where(lane == LANES - 1, pltpu.roll(near, 1, 0), near), 1, 1)
        east = pltpu.roll(jnp.where(lane == 0, pltpu.roll(near, chunks - 1, 0), near), LANES - 1, 1)
        return coef * (far + 2.0 * (west + east) - 8.0 * near), coef * near

    psi_ref[...] = inner_ref[...]
    north = near_far(north_ref[chunks:, :], north_ref[0:chunks, :], coef * has_north)
    south = near_far(south_ref[0:chunks, :], south_ref[chunks:, :], coef * has_south)
    for chunk in range(chunks):
        low = chunk + (PAIR - 1) * chunks
        for row in range(2):
            here = slice(row, row + 1)
            psi_ref[chunk, here, :] = inner_ref[chunk, here, :] - north[row][chunk : chunk + 1]
            here = slice(cells - 1 - row, cells - row)
            psi_ref[low, here, :] = inner_ref[low, here, :] - south[row][chunk : chunk + 1]


def vertical_kernel(lower_ref, upper_ref, inverse_ref, psi_ref, out_ref, held_ref, sem):
    fcount, levels, cells, _ = held_ref.shape
    step = 16
    copies = []
    swap = swapped()
    for field in range(fcount):
        source = lax.bitwise_xor(field, swap * (fcount // PAIR)) * levels
        for first in range(0, cells, step):
            rows = slice(first, first + step)
            sweep = []
            for level in range(levels):
                rhs = psi_ref[source + level, rows, :]
                if level:
                    rhs = rhs + lower_ref[field, level] * sweep[-1]
                sweep.append(rhs * inverse_ref[field, level])
            value = sweep[-1]
            held_ref[field, levels - 1, rows, :] = value
            for level in range(levels - 2, -1, -1):
                value = sweep[level] - upper_ref[field, level] * value
                held_ref[field, level, rows, :] = value
        copy = pltpu.make_async_copy(held_ref.at[field], out_ref.at[field], sem.at[field])
        copy.start()
        copies.append(copy)
    for copy in copies:
        copy.wait()


def vertical_tables(vert_coef):
    fcount = vert_coef.shape[0]
    levels = vert_coef.shape[1] + 1
    zero_column = jnp.zeros((fcount, 1), jnp.float32)
    lower_coef = jnp.concatenate([zero_column, vert_coef], axis=1)
    upper_coef = jnp.concatenate([vert_coef, zero_column], axis=1)
    diagonal = 1.0 + lower_coef + upper_coef
    uppers, inverses = [], []
    for level in range(levels):
        denominator = diagonal[:, level]
        if level:
            denominator = denominator + lower_coef[:, level] * uppers[-1]
        inverses.append(1.0 / denominator)
        uppers.append(-upper_coef[:, level] / denominator)
    return lower_coef, jnp.stack(uppers, axis=1), jnp.stack(inverses, axis=1)


SMEM = pltpu.MemorySpace.SMEM
VMEM = pltpu.MemorySpace.VMEM


def smem():
    return pl.BlockSpec(memory_space=SMEM)


def vmem():
    return pl.BlockSpec(memory_space=VMEM)


def anywhere():
    return pl.BlockSpec(memory_space=pl.ANY)


def body(fields, hyper_coef, vert_coef, dep_owner, dep_row, dep_col, shifts, fracs):
    fcount, levels, cells, width = fields.shape
    count = fcount * levels
    chunks = lax.axis_size("lon")
    groups = lax.axis_size("group")
    tile_rows = cells // TILE
    tile_cols = width // TILE
    tiles = tile_rows * tile_cols
    rows = PAIR * cells
    f32 = jnp.float32
    limit = pltpu.CompilerParams(vmem_limit_bytes=48 * 1024 * 1024)

    table = jnp.concatenate(
        [
            dep_owner.reshape(1, tiles),
            dep_row.reshape(1, tiles),
            dep_col.reshape(1, tiles),
            shifts.reshape(tiles, 2).T,
            fracs.reshape(tiles, 2).T,
        ],
        axis=0,
    )
    flat = fields.reshape(count, cells, width)
    blocks = pl.pallas_call(
        pack_border_kernel,
        out_shape=jax.ShapeDtypeStruct((count, TILE, width), f32),
        in_specs=[anywhere()],
        out_specs=vmem(),
        scratch_shapes=[pltpu.SemaphoreType.DMA((PAIR,))],
        compiler_params=limit,
        name="pack_border",
    )(flat)
    rest = pl.pallas_call(
        functools.partial(pack_inner_kernel, tile_rows, tile_cols, groups * PAIR * tile_rows - 2),
        out_shape=jax.ShapeDtypeStruct((count, cells - TILE + INFO_ROWS, width), f32),
        in_specs=[anywhere(), vmem()],
        out_specs=vmem(),
        scratch_shapes=[pltpu.VMEM((8, LANES), jnp.int32), pltpu.SemaphoreType.DMA((PAIR,))],
        compiler_params=limit,
        name="pack_inner",
    )(flat, table)
    blocks = lax.all_to_all(blocks, ("part", "lon"), 0, 0, tiled=True)
    blocks, rest, vert_coef = lax.optimization_barrier((blocks, rest, vert_coef))
    rest = lax.all_to_all(rest, ("part", "lon"), 0, 0, tiled=True)
    tables = vertical_tables(vert_coef)
    ready, tables = lax.optimization_barrier((blocks, tables))
    southward = [
        (group * PAIR + part, (group + 1) % groups * PAIR + PAIR - 1 - part) for group in range(groups) for part in range(PAIR)
    ]
    northward = [(target, source) for source, target in southward]
    bands = ("group", "part")
    north = lax.ppermute(ready[(PAIR - 1) * chunks :, :TILE, :], bands, southward)
    south = lax.ppermute(ready[:chunks, :TILE, :], bands, northward)
    places = rest[:, cells - TILE, tiles : 5 * tiles].astype(jnp.int32)
    edge = jax.ShapeDtypeStruct((2 * chunks, width), f32)
    phi, top, bottom = pl.pallas_call(
        interpolate_kernel,
        out_shape=(jax.ShapeDtypeStruct((chunks, rows + 2 * PAD, width), f32), edge, edge),
        in_specs=[smem()] + [vmem()] * 5,
        out_specs=(vmem(), vmem(), vmem()),
        scratch_shapes=[
            pltpu.VMEM((chunks, rows + 2 * TILE + 8, width), f32),
            pltpu.VMEM((min(16, chunks) * tile_rows, SPAN, width), f32),
            pltpu.SemaphoreType.DMA((2 + 2 * PAIR,)),
        ],
        compiler_params=limit,
        name="interpolate",
    )(places, blocks, rest, north, south, tap_matrix())
    above = lax.ppermute(bottom, bands, southward)
    below = lax.ppermute(top, bands, northward)
    psi_shape = jax.ShapeDtypeStruct((count, cells, width), f32)
    inner = pl.pallas_call(
        functools.partial(diffuse_kernel, groups),
        out_shape=psi_shape,
        in_specs=[smem(), vmem(), vmem()],
        out_specs=vmem(),
        scratch_shapes=[
            pltpu.VMEM((chunks, rows + 2 * PAD, width), f32),
            pltpu.VMEM((chunks, rows, width), jnp.bfloat16),
            pltpu.VMEM((chunks, rows, width), jnp.bfloat16),
        ],
        compiler_params=limit,
        name="diffuse",
    )(hyper_coef, phi, beside_matrix())
    psi = pl.pallas_call(
        functools.partial(mend_kernel, groups),
        out_shape=psi_shape,
        in_specs=[smem(), vmem(), vmem(), vmem()],
        out_specs=vmem(),
        compiler_params=limit,
        name="mend",
    )(hyper_coef, above, below, inner)
    psi = lax.all_to_all(psi, ("part", "lon"), 0, 0, tiled=True)
    return pl.pallas_call(
        vertical_kernel,
        out_shape=jax.ShapeDtypeStruct((fcount, levels, cells, width), f32),
        in_specs=[smem(), smem(), smem(), vmem()],
        out_specs=anywhere(),
        scratch_shapes=[pltpu.VMEM((fcount, levels, cells, width), f32), pltpu.SemaphoreType.DMA((fcount,))],
        compiler_params=limit,
        name="solve",
    )(*tables, psi)


def solution(mesh):
    lat, lon = mesh.shape["lat"], mesh.shape["lon"]
    grouped = Mesh(mesh.devices.reshape(lat // PAIR, PAIR, lon), ("group", "part", "lon"))
    bands = ("group", "part")
    cells = P(None, None, bands, "lon")
    tiles = P(bands, "lon", None, None)
    return jax.shard_map(
        body,
        mesh=grouped,
        in_specs=(cells, P(), P(), tiles, tiles, tiles, tiles, tiles),
        out_specs=cells,
        check_vma=False,
    )
```
